32 devices in a mesh: dp: 32 (over z, y, x, core).
Axes of the slice: x: 2, y: 2, z: 4, core: 2. Of those that a mesh axis runs over, the one named last changes fastest.
Arguments:
- tokens: bfloat16 [49152, 768], P('dp'), may hold values from -6 to 6
- buckets: int32 [128], P('dp'), may hold values from 0 to 2, as said below
- lengths: int32 [128], P('dp'), may hold values from 88 to 384, as said below
- w_query: bfloat16 [768, 768], P('dp'), may hold values from -0.21875 to 0.21875
- w_key: bfloat16 [768, 768], P('dp'), may hold values from -0.21875 to 0.21875
- w_value: bfloat16 [768, 768], P('dp'), may hold values from -0.21875 to 0.21875
- w_output: bfloat16 [768, 768], P('dp'), may hold values from -2 to 2
- bias_query: bfloat16 [768], P('dp'), may hold values from -3 to 3
- bias_value: bfloat16 [768], P('dp'), may hold values from -3 to 3
- bias_output: bfloat16 [768], P('dp'), may hold values from -3 to 3
- gain_first: bfloat16 [768], P('dp'), may hold values from 0.5 to 1.5
- shift_first: bfloat16 [768], P('dp'), may hold values from -2 to 2
- w_expand: bfloat16 [768, 3072], P('dp'), may hold values from -0.21875 to 0.21875
- bias_expand: bfloat16 [3072], P('dp'), may hold values from -3 to 3
- w_shrink: bfloat16 [3072, 768], P('dp'), may hold values from -0.15625 to 0.15625
- bias_shrink: bfloat16 [768], P('dp'), may hold values from -3 to 3
- gain_second: bfloat16 [768], P('dp'), may hold values from 0.5 to 1.5
- shift_second: bfloat16 [768], P('dp'), may hold values from -2 to 2
- grad_out: bfloat16 [49152, 768], P('dp'), may hold values from -6 to 6
Outputs:
- layer_out: bfloat16 [49152, 768], P('dp')
- grad_tokens: float32 [49152, 768], P('dp')
- grad_w_query: float32 [768, 768], P('dp')
- grad_w_key: float32 [768, 768], P('dp')
- grad_w_value: float32 [768, 768], P('dp')
- grad_w_output: float32 [768, 768], P('dp')
- grad_bias_query: float32 [768], P('dp')
- grad_bias_value: float32 [768], P('dp')
- grad_bias_output: float32 [768], P('dp')
- grad_gain_first: float32 [768], P('dp')
- grad_shift_first: float32 [768], P('dp')
- grad_w_expand: float32 [768, 3072], P('dp')
- grad_bias_expand: float32 [3072], P('dp')
- grad_w_shrink: float32 [3072, 768], P('dp')
- grad_bias_shrink: float32 [768], P('dp')
- grad_gain_second: float32 [768], P('dp')
- grad_shift_second: float32 [768], P('dp')
The draws below stay inside these ranges and needn't reach their ends.
Inputs may be any that keep to these rules, and one draw needn't show every extreme that they name: `buckets`: bucket of each sequence: 0, 1 or 2 for 176, 224 or 384 rows; a sequence fills the first rows of its slot of 384 rows. `lengths`: true length of each sequence: at least half of its bucket's rows (rounded down), at most all of them; keys at or past it are padding.
All inputs are finite; a program needn't handle non-finite values.
Results may differ from the reference program's by a relative error of at most 0.014.
The reference program's roundings to bfloat16 on the way count: a program that leaves them out, or rounds other values in their place, can miss the bound.
Values may be sent and summed in bfloat16 or wider, within the bound.
No kernel may reach another device: no remote copies, remote signals or barrier semaphores. Data moves between devices by JAX's collectives and lax.ppermute only.
A program may use at most 256 MiB of HBM per device.

```python
import math
import jax
import jax.numpy as jnp
from jax import lax

D = 768
H = 12
HD = 64
FF = 3072
B0 = 176
B1 = 224
B2 = 384
SEQS = 128
ROWS = 49152


def bucket_core(key):
    bucket_ids = jax.random.randint(jax.random.fold_in(key, 11), (SEQS,), 0, 3)
    full_index = jax.random.randint(jax.random.fold_in(key, 12), (), 0, SEQS)
    slot_ids = jnp.arange(SEQS)
    chosen = slot_ids == full_index
    shortest = slot_ids == (full_index + 1) % SEQS
    bucket_ids = jnp.where(chosen, 2, jnp.where(shortest, 0, bucket_ids))
    return (bucket_ids, chosen, shortest)


def draw_buckets(key, part):
    bucket_ids, chosen, shortest = bucket_core(key)
    return bucket_ids.astype(jnp.int32)


def draw_lengths(key, part):
    bucket_ids, chosen, shortest = bucket_core(key)
    key = jax.random.fold_in(key, 5)
    bucket_rows = jnp.where(bucket_ids == 0, B0, jnp.where(bucket_ids == 1, B1, B2))
    drawn = jax.random.randint(key, (SEQS,), bucket_rows // 2, bucket_rows + 1)
    drawn = jnp.where(shortest, B0 // 2, drawn)
    return jnp.where(chosen, B2, drawn).astype(jnp.int32)


def spiked(array, rng, source, target, blocks, factor):
    def block_of(position):
        return (jnp.arange(array.shape[position]) // (array.shape[position] // blocks)).reshape((-1,) + (1,) * (array.ndim - 1 - position))

    first = jax.random.permutation(rng, blocks)[block_of(target)]
    far = (block_of(target) + blocks // 2) % blocks
    return jnp.where((block_of(source) == first) | (block_of(source) == far), factor * array, array)


def block_scale(key, dims, cuts, least, high):
    def one(axis_at, parts):
        heights = jax.random.uniform(jax.random.fold_in(jax.random.fold_in(key, 6), axis_at), (parts,), jnp.float32, least / len(cuts), high / len(cuts))
        return jnp.repeat(jnp.exp(heights), dims[axis_at] // parts).reshape((-1,) + (1,) * (len(dims) - axis_at - 1))

    factor_of = one(*cuts[0])
    for cut in cuts[1:]:
        factor_of = factor_of * one(*cut)
    return factor_of


def scatter_about(stream_key, shape, scale, most, cuts=(), kind=jnp.bfloat16):
    result = scale * jax.random.normal(stream_key, shape, jnp.float32)
    if cuts:
        result = result * block_scale(stream_key, shape, cuts, -0.22, 0.18)
    return jnp.clip(result, -most, most).astype(kind)


def heavy_noise(stream_key, extent, spread, bound, cuts, heavy, kind=jnp.bfloat16):
    values = spread * jax.random.normal(stream_key, extent, jnp.float32)
    if cuts:
        values = values * block_scale(stream_key, extent, cuts, -0.22, 0.18)
    return jnp.clip(spiked(values, jax.random.fold_in(stream_key, 3), *heavy), -bound, bound).astype(kind)


def setup_inputs(seed: int = 0) -> dict:
    keys = jax.random.split(jax.random.key(seed), 20)
    tokens = heavy_noise(keys[0], (ROWS, D), 1.0, 6.0, ((0, 32),), (0, 1, 32, 2.75))
    buckets = draw_buckets(jax.random.fold_in(keys[19], 71), 0)
    lengths = draw_lengths(jax.random.fold_in(keys[19], 71), 0)
    w_query = scatter_about(keys[3], (D, D), D ** -0.5, 0.21875, ((0, 32),))
    w_key = scatter_about(keys[4], (D, D), D ** -0.5, 0.21875, ((0, 32),))
    w_value = scatter_about(keys[5], (D, D), D ** -0.5, 0.21875, ((0, 32),))
    w_output = scatter_about(keys[6], (D, D), (max(1, D * 4 // B2)) ** -0.5, 2.0, ((0, 32),))
    bias_query = scatter_about(keys[7], (D,), 0.5, 3.0, ((0, 32),))
    bias_value = scatter_about(keys[8], (D,), 0.5, 3.0, ((0, 32),))
    bias_output = scatter_about(keys[9], (D,), 0.5, 3.0, ((0, 32),))
    gain_first = jnp.clip(1.0 + 0.1 * jax.random.normal(keys[10], (D,), jnp.float32), 0.5, 1.5).astype(jnp.bfloat16)
    shift_first = scatter_about(keys[11], (D,), 0.3, 2.0, ((0, 32),))
    w_expand = scatter_about(keys[12], (D, FF), D ** -0.5, 0.21875, ((0, 32),))
    bias_expand = scatter_about(keys[13], (FF,), 0.5, 3.0, ((0, 32),))
    w_shrink = scatter_about(keys[14], (FF, D), (FF // 2) ** -0.5, 0.15625, ((0, 32),))
    bias_shrink = scatter_about(keys[15], (D,), 0.5, 3.0, ((0, 32),))
    gain_second = jnp.clip(1.0 + 0.1 * jax.random.normal(keys[16], (D,), jnp.float32), 0.5, 1.5).astype(jnp.bfloat16)
    shift_second = scatter_about(keys[17], (D,), 0.3, 2.0, ((0, 32),))
    grad_out = scatter_about(keys[18], (ROWS, D), 1.0, 6.0, ((0, 32),))
    return {"tokens": tokens, "buckets": buckets, "lengths": lengths, "w_query": w_query, "w_key": w_key, "w_value": w_value, "w_output": w_output, "bias_query": bias_query, "bias_value": bias_value, "bias_output": bias_output, "gain_first": gain_first, "shift_first": shift_first, "w_expand": w_expand, "bias_expand": bias_expand, "w_shrink": w_shrink, "bias_shrink": bias_shrink, "gain_second": gain_second, "shift_second": shift_second, "grad_out": grad_out}


epsilon = 1e-12
highest = lax.Precision.HIGHEST

@jax.custom_vjp
def low(v):
    return lax.optimization_barrier(v.astype(jnp.bfloat16)).astype(jnp.float32)

@jax.custom_vjp
def low_back(v):
    return v

def low_keep(v):
    return (low(v), None)

def low_pass(kept, grad):
    return (grad,)

def back_keep(v):
    return (v, None)

def back_low(kept, grad):
    return (low(grad),)
low.defvjp(low_keep, low_pass)
low_back.defvjp(back_keep, back_low)

def layer_norm(hidden, gain_vec, shift_vec):
    row_mean = lax.optimization_barrier(jnp.mean(hidden, -1, keepdims=True))
    centred = hidden - row_mean
    variance = lax.optimization_barrier(jnp.mean(centred * centred, -1, keepdims=True))
    return centred * lax.rsqrt(variance + epsilon) * gain_vec + shift_vec

def project(inputs, matrix):
    return jnp.einsum('gld,de->gle', inputs, matrix, precision=highest)

def layer_forward(weights, inputs, row_mask, key_mask):
    w_query, w_key, w_value, w_output, bias_query, bias_value, bias_output, gain_first, shift_first, w_expand, bias_expand, w_shrink, bias_shrink, gain_second, shift_second = weights
    group_size = inputs.shape[0]
    length = inputs.shape[1]
    queries = low_back(low(project(inputs, w_query) + bias_query)).reshape(group_size, length, H, HD)
    key_rows = low_back(low(project(inputs, w_key))).reshape(group_size, length, H, HD)
    value_rows = low_back(low(project(inputs, w_value) + bias_value)).reshape(group_size, length, H, HD)
    scores = jnp.einsum('gihe,gjhe->ghij', queries, key_rows, precision=highest) * (1.0 / math.sqrt(HD))
    scores = low_back(scores)
    scores = jnp.where(key_mask[:, None, None, :], scores, -1e+30)
    row_peak = lax.optimization_barrier(jnp.max(scores, -1, keepdims=True))
    exp_terms = jnp.exp(scores - row_peak)
    soft_weights = low(exp_terms / lax.optimization_barrier(jnp.sum(exp_terms, -1, keepdims=True)))
    context = jnp.einsum('ghij,gjhe->gihe', soft_weights, value_rows, precision=highest)
    context = low_back(low(context.reshape(group_size, length, D)))
    attended = low_back(project(context, w_output) + bias_output)
    first = layer_norm(inputs + attended, gain_first, shift_first)
    expand = low_back(project(low(first), w_expand) + bias_expand)
    active = low(jax.nn.gelu(expand, approximate=False))
    shrink = low_back(project(active, w_shrink) + bias_shrink)
    return layer_norm(first + shrink, gain_second, shift_second) * row_mask[:, :, None]

def reference(tokens, buckets, lengths, w_query, w_key, w_value, w_output, bias_query, bias_value, bias_output, gain_first, shift_first, w_expand, bias_expand, w_shrink, bias_shrink, gain_second, shift_second, grad_out):
    weights = tuple((item.astype(jnp.float32) for item in (w_query, w_key, w_value, w_output, bias_query, bias_value, bias_output, gain_first, shift_first, w_expand, bias_expand, w_shrink, bias_shrink, gain_second, shift_second)))
    group_count = SEQS // 8
    bucket_rows = jnp.where(buckets == 0, B0, jnp.where(buckets == 1, B1, B2)).astype(jnp.int32)
    positions = jnp.arange(B2, dtype=jnp.int32)
    row_mask = (positions[None, :] < bucket_rows[:, None]).astype(jnp.float32).reshape(group_count, 8, B2)
    key_mask = (positions[None, :] < lengths[:, None]).reshape(group_count, 8, B2)
    inputs = tokens.astype(jnp.float32).reshape(group_count, 8, B2, D)
    cotangent = grad_out.astype(jnp.float32).reshape(group_count, 8, B2, D)

    def group_step(summed, pieces):
        group_in, group_rows, group_keys, group_cot = pieces
        output, pullback = jax.vjp(lambda params, values: layer_forward(params, values, group_rows, group_keys), weights, group_in)
        grad_params, grad_inputs = pullback(group_cot)
        return (tuple((left + right for left, right in zip(summed, grad_params))), (output, grad_inputs))
    zero_grads = tuple((jnp.zeros_like(item) for item in weights))
    summed, (outputs, grad_rows) = lax.scan(group_step, zero_grads, (inputs, row_mask, key_mask, cotangent))
    return (outputs.reshape(ROWS, D).astype(jnp.bfloat16), grad_rows.reshape(ROWS, D), summed[0], summed[1], summed[2], summed[3], summed[4], summed[5], summed[6], summed[7], summed[8], summed[9], summed[10], summed[11], summed[12], summed[13], summed[14])
```

```python
import functools, math
import jax, jax.numpy as jnp
from jax import lax
from jax.experimental import pallas as pl
from jax.experimental.pallas import tpu as pltpu
from jax.sharding import PartitionSpec as P
BF=jnp.bfloat16; F32=jnp.float32
D=768; HD=64; PAIRS=6
VM=58<<20
NEG=-1e30
def mm(a,b): return lax.dot_general(a,b,(((1,),(0,)),((),())),preferred_element_type=F32)
def nt(a,b): return lax.dot_general(a,b,(((1,),(1,)),((),())),preferred_element_type=F32)
def tn(a,b): return lax.dot_general(a,b,(((0,),(0,)),((),())),preferred_element_type=F32)
def lanes(rows,n=128): return lax.broadcasted_iota(jnp.int32,(rows,n),1)

def attn_fwd_kernel(len_ref, x_ref, wq_ref, wk_ref, wv_ref, sp_ref, q_ref, k_ref, v_ref, c_ref, e_ref):
    L=x_ref.shape[0]
    s=pl.program_id(0)
    n=len_ref[s]
    x=x_ref[...]
    q=(mm(x,wq_ref[...])+sp_ref[6:7].astype(F32)).astype(BF)
    k=mm(x,wk_ref[...]).astype(BF)
    v=(mm(x,wv_ref[...])+sp_ref[7:8].astype(F32)).astype(BF)
    q_ref[...]=q; k_ref[...]=k; v_ref[...]=v
    ln=lanes(L)
    even=ln<64
    row=lax.broadcasted_iota(jnp.int32,(L,128),0)
    kx=jnp.where((ln==0)&(row>=n),NEG,0.0).astype(BF)
    qx=jnp.where(ln==0,1.0,0.0).astype(BF)
    one_e=jnp.where(even,1.0,0.0).astype(BF)
    one_o=jnp.where(even,0.0,1.0).astype(BF)
    zero=jnp.zeros((L,128),BF)
    mt=jnp.zeros((L,128),F32); lt=jnp.ones((L,128),F32)
    for t in range(PAIRS):
        cs=slice(128*t,128*t+128)
        qp=q[:,cs]*jnp.asarray(0.125,BF); kp=k[:,cs]; vp=v[:,cs]
        ke=jnp.concatenate([kp,kx],1)
        ps=[];ms=[]
        for o in (0,1):
            qm=jnp.where(even if o==0 else ~even, qp, zero)
            sc=nt(jnp.concatenate([qm,qx],1),ke)
            m=jnp.max(sc,1,keepdims=True)
            ps.append(jnp.exp(sc-m).astype(BF)); ms.append(m)
        vv=jnp.concatenate([jnp.concatenate([jnp.where(even,vp,zero),one_e],1),
                            jnp.concatenate([jnp.where(even,zero,vp),one_o],1)],0)
        r=mm(jnp.concatenate(ps,1),vv)
        lb=r[:,128:]
        c_ref[:,cs]=(r[:,:128]/lb).astype(BF)
        sel_e=ln==t; sel_o=ln==64+t
        mt=jnp.where(sel_e,ms[0],jnp.where(sel_o,ms[1],mt))
        lt=jnp.where(sel_e|sel_o,lb,lt)
    neg=-(mt+jnp.log(lt))
    hi=neg.astype(BF); r1=neg-hi.astype(F32)
    mid=r1.astype(BF); lo=(r1-mid.astype(F32)).astype(BF)
    use=(ln%64)<PAIRS
    z=jnp.zeros((L,128),F32)
    e=jnp.where(use,hi.astype(F32),z)+pltpu.roll(jnp.where(use,mid.astype(F32),z),8,1)+pltpu.roll(jnp.where(use,lo.astype(F32),z),16,1)
    e=jnp.where(ln==24,1.0,e)
    e_ref[...]=e.astype(BF)

def attn_fwd(lengths,x,wq,wk,wv,sp):
    S=lengths.shape[0]; R=x.shape[0]; L=R//S
    rowb=pl.BlockSpec((L,D),lambda s,*_:(s,0))
    w=pl.BlockSpec((D,D),lambda s,*_:(0,0))
    b=pl.BlockSpec((8,D),lambda s,*_:(0,0))
    return pl.pallas_call(attn_fwd_kernel,
        grid_spec=pltpu.PrefetchScalarGridSpec(num_scalar_prefetch=1,grid=(S,),
            in_specs=[rowb,w,w,w,b],
            out_specs=[rowb,rowb,rowb,rowb,pl.BlockSpec((L,128),lambda s,*_:(s,0))]),
        out_shape=[jax.ShapeDtypeStruct((R,D),BF)]*4+[jax.ShapeDtypeStruct((R,128),BF)],
        compiler_params=pltpu.CompilerParams(vmem_limit_bytes=VM),
        cost_estimate=pl.CostEstimate(flops=9_000_000_000,bytes_accessed=20_000_000,transcendentals=7_000_000),
        name="attn_fwd")(lengths,x,wq,wk,wv,sp)

def attn_bwd_kernel(len_ref, q_ref, k_ref, v_ref, c_ref, e_ref, g_ref, dq_ref, dk_ref, dv_ref, sm_ref):
    L=q_ref.shape[0]
    s=pl.program_id(0)
    n=len_ref[s]
    ln=lanes(L); even=ln<64
    row=lax.broadcasted_iota(jnp.int32,(L,128),0)
    eq=e_ref[...]
    mask=(ln==24)&(row>=n)
    zero=jnp.zeros((L,128),BF); zf=jnp.zeros((L,128),F32)
    scale=jnp.asarray(0.125,BF)
    kbase=jnp.where(mask,NEG,0.0)
    for t in range(PAIRS):
        cs=slice(128*t,128*t+128)
        q=q_ref[:,cs]; k=k_ref[:,cs]; v=v_ref[:,cs]; g=g_ref[:,cs]
        qs=q*scale
        gc=g.astype(F32)*c_ref[:,cs].astype(F32)
        ps=[];ss=[]
        for o in (0,1):
            sel=even if o==0 else ~even
            d=jnp.sum(jnp.where(sel,gc,zf),1,keepdims=True)
            dh=d.astype(BF).astype(F32); dl=d-dh
            gx=jnp.where(ln==0,-dh,jnp.where(ln==1,-dl,zf)).astype(BF)
            base=64*o+t
            hot=(ln==base)|(ln==base+8)|(ln==base+16)
            kx=jnp.where(hot,1.0,kbase).astype(BF)
            vx=jnp.where(ln<2,1.0,0.0).astype(BF)
            sc=nt(jnp.concatenate([jnp.where(sel,qs,zero),eq],1),jnp.concatenate([k,kx],1))
            p=jnp.exp(sc)
            dp=nt(jnp.concatenate([jnp.where(sel,g,zero),gx],1),jnp.concatenate([v,vx],1))
            ds=(p*dp).astype(BF)
            ps.append(p.astype(BF)); ss.append(ds)
        kk=jnp.concatenate([jnp.where(even,k,zero),jnp.where(even,zero,k)],0)
        dq_ref[:,cs]=(mm(jnp.concatenate(ss,1),kk)*0.125).astype(BF)
        qq=jnp.concatenate([jnp.where(even,q,zero),jnp.where(even,zero,q)],0)
        gg=jnp.concatenate([jnp.where(even,g,zero),jnp.where(even,zero,g)],0)
        dk_ref[:,cs]=(tn(jnp.concatenate(ss,0),qq)*0.125).astype(BF)
        dv_ref[:,cs]=tn(jnp.concatenate(ps,0),gg).astype(BF)
    u=jnp.concatenate([colsum(dq_ref[...].astype(F32)),colsum(dv_ref[...].astype(F32)),jnp.zeros((6,D),F32)],0)
    @pl.when(s==0)
    def _(): sm_ref[...]=u
    @pl.when(s>0)
    def _(): sm_ref[...]+=u

def attn_bwd(lengths,q,k,v,c,e,g):
    S=lengths.shape[0]; R=q.shape[0]; L=R//S
    rowb=pl.BlockSpec((L,D),lambda s,*_:(s,0))
    w=pl.BlockSpec((D,D),lambda s,*_:(0,0))
    return pl.pallas_call(attn_bwd_kernel,
        grid_spec=pltpu.PrefetchScalarGridSpec(num_scalar_prefetch=1,grid=(S,),
            in_specs=[rowb,rowb,rowb,rowb,pl.BlockSpec((L,128),lambda s,*_:(s,0)),rowb],
            out_specs=[rowb,rowb,rowb,pl.BlockSpec((8,D),lambda s,*_:(0,0))]),
        out_shape=[jax.ShapeDtypeStruct((R,D),BF)]*3+[jax.ShapeDtypeStruct((8,D),F32)],
        compiler_params=pltpu.CompilerParams(vmem_limit_bytes=VM),
        cost_estimate=pl.CostEstimate(flops=15_000_000_000,bytes_accessed=24_000_000,transcendentals=7_000_000),
        name="attn_bwd")(lengths,q,k,v,c,e,g)

EPS=1e-12
def gelu_parts(v):
    a=jnp.abs(v)
    d=1.0+a*(0.3275911*math.sqrt(0.5))
    t=pl.reciprocal(d,approx=True)
    t=t*(2.0-d*t)
    ex=jnp.exp(v*v*-0.5)
    po=((((1.061405429*0.5*t-1.453152027*0.5)*t+1.421413741*0.5)*t-0.284496736*0.5)*t+0.254829592*0.5)*t
    tail=po*ex
    phi=jnp.where(v>=0,1.0-tail,tail)
    return v*phi, phi+v*(ex*(1.0/math.sqrt(2*math.pi)))
def ln_parts(h):
    mu=jnp.mean(h,1,keepdims=True); c=h-mu
    r=lax.rsqrt(jnp.mean(c*c,1,keepdims=True)+EPS)
    return c*r, r
def ln_back(up,n,r,gain):
    e=up*gain
    return r*(e-jnp.mean(e,1,keepdims=True)-n*jnp.mean(e*n,1,keepdims=True))
def colsum(x): return jnp.sum(x,0,keepdims=True)
FC=512
def ffn_fwd_kernel(bk_ref,x_ref,c_ref,go_ref,wo_ref,we_ref,ws_ref,sp_ref,be_ref,
        n1_ref,r1_ref,fl_ref,act_ref,gp_ref,out_ref,gh_ref,gs_ref,sm_ref):
    M=x_ref.shape[0]; FF=we_ref.shape[1]
    s=pl.program_id(0)
    sp=sp_ref[...].astype(F32)
    bo,g1,s1,bs,g2,s2=[sp[i:i+1] for i in range(6)]
    att=mm(c_ref[...],wo_ref[...])+bo
    n1,r1=ln_parts(x_ref[...].astype(F32)+att)
    n1_ref[...]=n1; r1_ref[...]=jnp.broadcast_to(r1,(M,128))
    first=n1*g1+s1
    fl=first.astype(BF); fl_ref[...]=fl
    acc=jnp.zeros((M,D),F32)
    for f in range(0,FF,FC):
        fs=slice(f,f+FC)
        ex=mm(fl,we_ref[:,fs])+be_ref[:,fs].astype(F32)
        a,gp=gelu_parts(ex)
        ab=a.astype(BF)
        act_ref[:,fs]=ab; gp_ref[:,fs]=gp.astype(BF)
        acc=acc+mm(ab,ws_ref[fs,:])
    n2,r2=ln_parts(first+(acc+bs))
    rows=jnp.where(bk_ref[s]==0,176,jnp.where(bk_ref[s]==1,224,384))
    rm=jnp.where(lax.broadcasted_iota(jnp.int32,(M,1),0)<rows,1.0,0.0)
    out_ref[...]=((n2*g2+s2)*rm).astype(BF)
    up=go_ref[...].astype(F32)*rm
    gh=ln_back(up,n2,r2,g2)
    gh_ref[...]=gh
    gs=gh.astype(BF); gs_ref[...]=gs
    u=jnp.concatenate([colsum(up*n2),colsum(up),colsum(gs.astype(F32)),jnp.zeros((5,D),F32)],0)
    @pl.when(s==0)
    def _(): sm_ref[...]=u
    @pl.when(s>0)
    def _(): sm_ref[...]+=u

def ffn_fwd(buckets,x,c,go,wo,we,ws,sp,be):
    S=buckets.shape[0]; R=x.shape[0]; M=R//S; FF=we.shape[1]
    rb=lambda n:pl.BlockSpec((M,n),lambda s,*_:(s,0))
    full=lambda a,b:pl.BlockSpec((a,b),lambda s,*_:(0,0))
    return pl.pallas_call(ffn_fwd_kernel,
        grid_spec=pltpu.PrefetchScalarGridSpec(num_scalar_prefetch=1,grid=(S,),
            in_specs=[rb(D),rb(D),rb(D),full(D,D),full(D,FF),full(FF,D),full(8,D),full(1,FF)],
            out_specs=[rb(D),rb(128),rb(D),rb(FF),rb(FF),rb(D),rb(D),rb(D),full(8,D)]),
        out_shape=[jax.ShapeDtypeStruct((R,D),F32),jax.ShapeDtypeStruct((R,128),F32),jax.ShapeDtypeStruct((R,D),BF),
            jax.ShapeDtypeStruct((R,FF),BF),jax.ShapeDtypeStruct((R,FF),BF),jax.ShapeDtypeStruct((R,D),BF),
            jax.ShapeDtypeStruct((R,D),F32),jax.ShapeDtypeStruct((R,D),BF),jax.ShapeDtypeStruct((8,D),F32)],
        compiler_params=pltpu.CompilerParams(vmem_limit_bytes=VM),
        cost_estimate=pl.CostEstimate(flops=17_000_000_000,bytes_accessed=60_000_000,transcendentals=9_000_000),
        name="ffn_fwd")(buckets,x,c,go,wo,we,ws,sp,be)

def ffn_bwd_kernel(gs_ref,gh_ref,gp_ref,n1_ref,r1_ref,wo_ref,we_ref,ws_ref,sp_ref,
        ge_ref,gr_ref,ga_ref,gc_ref,sm_ref,sb_ref):
    M=gs_ref.shape[0]; FF=we_ref.shape[1]
    s=pl.program_id(0)
    g1=sp_ref[1:2].astype(F32)
    gs=gs_ref[...]
    acc=gh_ref[...]
    bsum=[]
    for f in range(0,FF,FC):
        fs=slice(f,f+FC)
        ge=(nt(gs,ws_ref[fs,:])*gp_ref[:,fs].astype(F32)).astype(BF)
        ge_ref[:,fs]=ge
        bsum.append(colsum(ge.astype(F32)))
        acc=acc+nt(ge,we_ref[:,fs])
    n1=n1_ref[...]
    gr=ln_back(acc,n1,r1_ref[:,:1],g1)
    gr_ref[...]=gr
    ga=gr.astype(BF); ga_ref[...]=ga
    gc_ref[...]=nt(ga,wo_ref[...]).astype(BF)
    u=jnp.concatenate([colsum(ga.astype(F32)),colsum(acc*n1),colsum(acc),jnp.zeros((5,D),F32)],0)
    ub=jnp.concatenate(bsum,1)
    @pl.when(s==0)
    def _():
        sm_ref[...]=u; sb_ref[...]=ub
    @pl.when(s>0)
    def _():
        sm_ref[...]+=u; sb_ref[...]+=ub

def ffn_bwd(gs,gh,gp,n1,r1,wo,we,ws,sp,S):
    R=gs.shape[0]; M=R//S; FF=we.shape[1]
    rb=lambda n:pl.BlockSpec((M,n),lambda s:(s,0))
    full=lambda a,b:pl.BlockSpec((a,b),lambda s:(0,0))
    return pl.pallas_call(ffn_bwd_kernel,grid=(S,),
            in_specs=[rb(D),rb(D),rb(FF),rb(D),rb(128),full(D,D),full(D,FF),full(FF,D),full(8,D)],
            out_specs=[rb(FF),rb(D),rb(D),rb(D),full(8,D),full(1,FF)],
        out_shape=[jax.ShapeDtypeStruct((R,FF),BF),jax.ShapeDtypeStruct((R,D),F32),jax.ShapeDtypeStruct((R,D),BF),
            jax.ShapeDtypeStruct((R,D),BF),jax.ShapeDtypeStruct((8,D),F32),jax.ShapeDtypeStruct((1,FF),F32)],
        compiler_params=pltpu.CompilerParams(vmem_limit_bytes=VM),
        cost_estimate=pl.CostEstimate(flops=17_000_000_000,bytes_accessed=60_000_000,transcendentals=0),
        name="ffn_bwd")(gs,gh,gp,n1,r1,wo,we,ws,sp)

def tn_kernel(a_ref,b_ref,o_ref): o_ref[...]=tn(a_ref[...],b_ref[...]).astype(o_ref.dtype)
def grad_w(a,b,bm,bn,name,dt=BF,order=0):
    R,Ma=a.shape; Nb=b.shape[1]
    if order==0:
        grid=(Ma//bm,Nb//bn); ia=lambda i,j:(0,i); ib=lambda i,j:(0,j); io=lambda i,j:(i,j)
    else:
        grid=(Nb//bn,Ma//bm); ia=lambda j,i:(0,i); ib=lambda j,i:(0,j); io=lambda j,i:(i,j)
    return pl.pallas_call(tn_kernel,grid=grid,in_specs=[pl.BlockSpec((R,bm),ia),pl.BlockSpec((R,bn),ib)],
        out_specs=pl.BlockSpec((bm,bn),io),out_shape=jax.ShapeDtypeStruct((Ma,Nb),dt),
        compiler_params=pltpu.CompilerParams(vmem_limit_bytes=VM),
        cost_estimate=pl.CostEstimate(flops=2*R*Ma*Nb,bytes_accessed=2*R*(Ma+Nb)+2*Ma*Nb,transcendentals=0),
        name=name)(a,b)
def resid_kernel(gr_ref,a_ref,b_ref,c_ref,wa_ref,wb_ref,wc_ref,o_ref):
    o_ref[...]=gr_ref[...]+nt(a_ref[...],wa_ref[...])+nt(b_ref[...],wb_ref[...])+nt(c_ref[...],wc_ref[...])
def grad_in(gr,a,b,c,wa,wb,wc,S):
    R=gr.shape[0]; M=R//S
    rb=pl.BlockSpec((M,D),lambda s:(s,0)); w=pl.BlockSpec((D,D),lambda s:(0,0))
    return pl.pallas_call(resid_kernel,grid=(S,),in_specs=[rb]*4+[w]*3,out_specs=rb,
        out_shape=jax.ShapeDtypeStruct((R,D),F32),
        compiler_params=pltpu.CompilerParams(vmem_limit_bytes=VM),
        cost_estimate=pl.CostEstimate(flops=6*R*D*D,bytes_accessed=20_000_000,transcendentals=0),
        name="grad_in")(gr,a,b,c,wa,wb,wc)


def exchange(value, pairs):
    return lax.ppermute(value, "dp", pairs)


def flip(count, mask):
    return [(i, i ^ mask) for i in range(count)]


def turn(count, even_mask, odd_mask):
    return [(i, i ^ (odd_mask if i & 1 else even_mask)) for i in range(count)]


def gather_tree(block):
    along_z = jnp.stack([block] + [exchange(block, flip(32, 8 * k)) for k in (1, 2, 3)])
    near = exchange(along_z, turn(32, 2, 4))
    far = exchange(jnp.concatenate([along_z, near]), turn(32, 4, 2))
    mine = (along_z, near, far)
    return mine + tuple(exchange(piece, flip(32, 1)) for piece in mine)


def piece_owner(me, other_core, far, near, k):
    core = me & 1
    near_mask = 2 + 2 * (core ^ other_core)
    far_mask = 6 - near_mask
    return me ^ (other_core + far * far_mask + near * near_mask + 8 * k)


def unpack_kernel(cuts, me_ref, *refs):
    pieces, outs, sems = refs[:6], refs[6:-1], refs[-1]
    me = me_ref[0]
    for other in (0, 1):
        along_z, near, far = pieces[3 * other : 3 * other + 3]
        for k in range(4):
            for ref, at, owner in (
                (along_z, k, piece_owner(me, other, 0, 0, k)),
                (near, k, piece_owner(me, other, 0, 1, k)),
                (far, k, piece_owner(me, other, 1, 0, k)),
                (far, 4 + k, piece_owner(me, other, 1, 1, k)),
            ):
                for i, (start, rows) in enumerate(cuts):
                    pltpu.make_async_copy(
                        ref.at[at, pl.ds(start, rows)], outs[i].at[owner], sems.at[i]
                    ).start()
    for i, out in enumerate(outs):
        pltpu.make_async_copy(out, out, sems.at[i]).wait()


def unpack(me, pieces, heights, name):
    cuts = []
    start = 0
    for rows in heights:
        cuts.append((start, rows))
        start += rows
    anywhere = pl.BlockSpec(memory_space=pl.ANY)
    return pl.pallas_call(
        functools.partial(unpack_kernel, tuple(cuts)),
        grid_spec=pltpu.PrefetchScalarGridSpec(
            num_scalar_prefetch=1,
            grid=(1,),
            in_specs=[anywhere] * 6,
            out_specs=[anywhere] * len(cuts),
            scratch_shapes=[pltpu.SemaphoreType.DMA((len(cuts),))],
        ),
        out_shape=[jax.ShapeDtypeStruct((32, rows, D), BF) for rows in heights],
        compiler_params=pltpu.CompilerParams(vmem_limit_bytes=4 << 20),
        cost_estimate=pl.CostEstimate(
            flops=0, bytes_accessed=2 * 64 * D * start, transcendentals=0
        ),
        name=name,
    )(me, *pieces)


def pack_kernel(cuts, me_ref, *refs):
    sources, (keep, send, sems) = refs[:-3], refs[-3:]
    me = me_ref[0]
    for other, target in ((0, keep), (1, send)):
        for far in (0, 1):
            for near in (0, 1):
                for k in range(4):
                    owner = piece_owner(me, other, far, near, k)
                    for i, start, rows, column in cuts:
                        pltpu.make_async_copy(
                            sources[i].at[owner, :, pl.ds(column, D)],
                            target.at[8 * far + 4 * near + k, pl.ds(start, rows)],
                            sems.at[other],
                        ).start()
    for other, target in ((0, keep), (1, send)):
        pltpu.make_async_copy(target, target, sems.at[other]).wait()


def pack(me, sources, name):
    cuts = []
    start = 0
    for i, source in enumerate(sources):
        for column in range(0, source.shape[2], D):
            cuts.append((i, start, source.shape[1], column))
            start += source.shape[1]
    anywhere = pl.BlockSpec(memory_space=pl.ANY)
    return pl.pallas_call(
        functools.partial(pack_kernel, tuple(cuts)),
        grid_spec=pltpu.PrefetchScalarGridSpec(
            num_scalar_prefetch=1,
            grid=(1,),
            in_specs=[anywhere] * len(sources),
            out_specs=[anywhere] * 2,
            scratch_shapes=[pltpu.SemaphoreType.DMA((2,))],
        ),
        out_shape=[jax.ShapeDtypeStruct((16, start, D), BF)] * 2,
        compiler_params=pltpu.CompilerParams(vmem_limit_bytes=4 << 20),
        cost_estimate=pl.CostEstimate(
            flops=0, bytes_accessed=2 * 64 * D * start, transcendentals=0
        ),
        name=name,
    )(me, *sources)


def add_up(*parts):
    total = parts[0].astype(F32)
    for part in parts[1:]:
        total = total + part.astype(F32)
    return total


def scatter_tree(keep, send):
    came = exchange(send, flip(32, 1))
    low = add_up(keep[:8], came[:8]).astype(BF)
    high = add_up(keep[8:], came[8:]).astype(BF)
    came = exchange(high, turn(32, 4, 2))
    high = add_up(low[4:], came[4:]).astype(BF)
    low = add_up(low[:4], came[:4]).astype(BF)
    came = exchange(high, turn(32, 2, 4))
    sums = [add_up(low[k], came[k]).astype(BF) for k in range(4)]
    return add_up(sums[0], *[exchange(sums[k], flip(32, 8 * k)) for k in (1, 2, 3)])


def vector_row(vectors):
    row = jnp.concatenate(vectors)
    return jnp.pad(row[None], ((0, 7), (0, D - row.shape[0])))


def body(
    tokens,
    buckets,
    lengths,
    w_query,
    w_key,
    w_value,
    w_output,
    bias_query,
    bias_value,
    bias_output,
    gain_first,
    shift_first,
    w_expand,
    bias_expand,
    w_shrink,
    bias_shrink,
    gain_second,
    shift_second,
    grad_out,
    count,
):
    slots = buckets.shape[0]
    whole = lambda v: lax.all_gather(v, "dp", axis=0, tiled=True)
    short = (
        bias_output,
        gain_first,
        shift_first,
        bias_shrink,
        gain_second,
        shift_second,
        bias_query,
        bias_value,
    )
    tree = count == 32
    if tree:
        me = lax.axis_index("dp").astype(jnp.int32).reshape(1)
        first_block = jnp.concatenate(
            [w_query, w_key, w_value, vector_row(short + (bias_expand,))]
        )
        full_query, full_key, full_value, rows = unpack(
            me, gather_tree(first_block), (24, 24, 24, 8), "unpack_qkv"
        )
        full_query, full_key, full_value = [
            w.reshape(D, D) for w in (full_query, full_key, full_value)
        ]
        rows = rows[:, 0, :288]
        vectors = rows[:, :192].reshape(32, 8, 24).transpose(1, 0, 2).reshape(8, D)
        full_bias_expand = rows[:, 192:].reshape(1, 4 * D)
        full_output, full_shrink = unpack(
            me,
            gather_tree(jnp.concatenate([w_output, w_shrink])),
            (24, 96),
            "unpack_shrink",
        )
        full_output = full_output.reshape(D, D)
        full_shrink = full_shrink.reshape(4 * D, D)
        full_expand = whole(w_expand)
    else:
        full_query, full_key, full_value, full_output, full_expand, full_shrink = [
            whole(w) for w in (w_query, w_key, w_value, w_output, w_expand, w_shrink)
        ]
        vectors = jnp.stack([whole(v) for v in short])
        full_bias_expand = whole(bias_expand)[None]

    q, k, v, context, ends = attn_fwd(
        lengths, tokens, full_query, full_key, full_value, vectors
    )
    normed, root, first_low, active, slope, layer_out, grad_h2, grad_shrink, sums_a = ffn_fwd(
        buckets,
        tokens,
        context,
        grad_out,
        full_output,
        full_expand,
        full_shrink,
        vectors,
        full_bias_expand,
    )
    dw_shrink = grad_w(active, grad_shrink, 768, 768, "dw_shrink")
    grad_expand, grad_h1, grad_attended, grad_context, sums_b, d_bias_expand = ffn_bwd(
        grad_shrink,
        grad_h2,
        slope,
        normed,
        root,
        full_output,
        full_expand,
        full_shrink,
        vectors,
        slots,
    )
    dw_expand = grad_w(first_low, grad_expand, 768, 768, "dw_expand")
    dw_output = grad_w(context, grad_attended, 768, 384, "dw_output")
    dq, dk, dv, sums_c = attn_bwd(lengths, q, k, v, context, ends, grad_context)
    dw_query = grad_w(tokens, dq, 768, 384, "dw_query")
    dw_key = grad_w(tokens, dk, 768, 384, "dw_key")
    dw_value = grad_w(tokens, dv, 768, 384, "dw_value")
    grad_tokens = grad_in(
        grad_h1, dq, dk, dv, full_query, full_key, full_value, slots
    )
    sums = (
        sums_b[0],
        sums_b[1],
        sums_b[2],
        sums_a[2],
        sums_a[0],
        sums_a[1],
        sums_c[0],
        sums_c[1],
    )
    if tree:
        sum_shrink = scatter_tree(
            *pack(me, [dw_shrink.reshape(32, 96, D)], "pack_shrink")
        )
        sum_expand = scatter_tree(
            *pack(
                me,
                [dw_expand.reshape(32, 24, 4 * D), dw_output.reshape(32, 24, D)],
                "pack_expand",
            )
        )
        rows = jnp.stack(sums).reshape(8, 32, 24).transpose(1, 0, 2).reshape(32, 192)
        rows = jnp.concatenate([rows, d_bias_expand.reshape(32, 96)], 1).astype(BF)
        rows = jnp.pad(rows[:, None], ((0, 0), (0, 7), (0, D - 288)))
        sum_qkv = scatter_tree(
            *pack(
                me,
                [w.reshape(32, 24, D) for w in (dw_query, dw_key, dw_value)] + [rows],
                "pack_qkv",
            )
        )
        own_query, own_key, own_value = [sum_qkv[24 * i : 24 * i + 24] for i in range(3)]
        own_output = sum_expand[96:]
        own_expand = jnp.concatenate([sum_expand[24 * i : 24 * i + 24] for i in range(4)], 1)
        own_shrink = sum_shrink
        own_rows = sum_qkv[72]
        own_short = [own_rows[24 * i : 24 * i + 24] for i in range(8)]
        own_bias_expand = own_rows[192:288]
    else:
        owned = lambda v: lax.psum_scatter(
            v.astype(F32), "dp", scatter_dimension=0, tiled=True
        )
        own_query, own_key, own_value, own_output, own_expand, own_shrink = [
            owned(w)
            for w in (dw_query, dw_key, dw_value, dw_output, dw_expand, dw_shrink)
        ]
        own_short = [owned(v) for v in sums]
        own_bias_expand = owned(d_bias_expand[0])
    (
        own_bias_output,
        own_gain_first,
        own_shift_first,
        own_bias_shrink,
        own_gain_second,
        own_shift_second,
        own_bias_query,
        own_bias_value,
    ) = own_short
    return (
        layer_out,
        grad_tokens,
        own_query,
        own_key,
        own_value,
        own_output,
        own_bias_query,
        own_bias_value,
        own_bias_output,
        own_gain_first,
        own_shift_first,
        own_expand,
        own_bias_expand,
        own_shrink,
        own_bias_shrink,
        own_gain_second,
        own_shift_second,
    )


def solution(mesh):
    split = P("dp")
    wide = P("dp", None)
    return jax.shard_map(
        functools.partial(body, count=mesh.shape["dp"]),
        mesh=mesh,
        in_specs=(wide, split, split)
        + (wide,) * 4
        + (split,) * 5
        + (wide, split, wide, split, split, split, wide),
        out_specs=(wide,) * 6 + (split,) * 5 + (wide, split, wide, split, split, split),
        check_vma=False,
    )
```

```python
import functools, math
import jax, jax.numpy as jnp
from jax import lax
from jax.experimental import pallas as pl
from jax.experimental.pallas import tpu as pltpu
from jax.sharding import PartitionSpec as P
BF=jnp.bfloat16; F32=jnp.float32
D=768; HD=64; PAIRS=6
VM=58<<20
NEG=-1e30
def hbm(*arrays): return [pltpu.with_memory_space_constraint(a,pltpu.HBM) for a in arrays]
RESIDENT=pl.BlockSpec(memory_space=pltpu.VMEM)
def mm(a,b): return lax.dot_general(a,b,(((1,),(0,)),((),())),preferred_element_type=F32)
def nt(a,b): return lax.dot_general(a,b,(((1,),(1,)),((),())),preferred_element_type=F32)
def tn(a,b): return lax.dot_general(a,b,(((0,),(0,)),((),())),preferred_element_type=F32)
def lanes(rows,n=128): return lax.broadcasted_iota(jnp.int32,(rows,n),1)

def attn_fwd_kernel(lo, len_ref, x_ref, wq_ref, wk_ref, wv_ref, sp_ref, q_ref, k_ref, v_ref, c_ref, e_ref):
    L=x_ref.shape[0]
    n=len_ref[pl.program_id(0)+lo]
    x=x_ref[...]
    q=(mm(x,wq_ref[...])+sp_ref[6:7].astype(F32)).astype(BF)
    k=mm(x,wk_ref[...]).astype(BF)
    v=(mm(x,wv_ref[...])+sp_ref[7:8].astype(F32)).astype(BF)
    q_ref[...]=q; k_ref[...]=k; v_ref[...]=v
    ln=lanes(L)
    even=ln<64
    row=lax.broadcasted_iota(jnp.int32,(L,128),0)
    kx=jnp.where((ln==0)&(row>=n),NEG,0.0).astype(BF)
    qx=jnp.where(ln==0,1.0,0.0).astype(BF)
    one_e=jnp.where(even,1.0,0.0).astype(BF)
    one_o=jnp.where(even,0.0,1.0).astype(BF)
    zero=jnp.zeros((L,128),BF)
    mt=jnp.zeros((L,128),F32); lt=jnp.ones((L,128),F32)
    for t in range(PAIRS):
        cs=slice(128*t,128*t+128)
        qp=q[:,cs]*jnp.asarray(0.125,BF); kp=k[:,cs]; vp=v[:,cs]
        ke=jnp.concatenate([kp,kx],1)
        ps=[];ms=[]
        for o in (0,1):
            qm=jnp.where(even if o==0 else ~even, qp, zero)
            sc=nt(jnp.concatenate([qm,qx],1),ke)
            m=jnp.max(sc,1,keepdims=True)
            ps.append(jnp.exp(sc-m).astype(BF)); ms.append(m)
        vv=jnp.concatenate([jnp.concatenate([jnp.where(even,vp,zero),one_e],1),
                            jnp.concatenate([jnp.where(even,zero,vp),one_o],1)],0)
        r=mm(jnp.concatenate(ps,1),vv)
        lb=r[:,128:]
        c_ref[:,cs]=(r[:,:128]/lb).astype(BF)
        sel_e=ln==t; sel_o=ln==64+t
        mt=jnp.where(sel_e,ms[0],jnp.where(sel_o,ms[1],mt))
        lt=jnp.where(sel_e|sel_o,lb,lt)
    neg=-(mt+jnp.log(lt))
    hi=neg.astype(BF); r1=neg-hi.astype(F32)
    mid=r1.astype(BF); rest=(r1-mid.astype(F32)).astype(BF)
    use=(ln%64)<PAIRS
    z=jnp.zeros((L,128),F32)
    e=jnp.where(use,hi.astype(F32),z)+pltpu.roll(jnp.where(use,mid.astype(F32),z),8,1)+pltpu.roll(jnp.where(use,rest.astype(F32),z),16,1)
    e=jnp.where(ln==24,1.0,e)
    e_ref[...]=e.astype(BF)

def over_slots(kernel,nin,lo,before):
    n=len(before)
    def run(*refs): kernel(lo,*refs[:nin],*refs[nin+n:])
    return run,[pl.BlockSpec(memory_space=pl.ANY)]*n,{nin+i:i for i in range(n)}

def attn_fwd(lengths,x,wq,wk,wv,sp,lo,hi,before=()):
    S=lengths.shape[0]; R=x.shape[0]; L=R//S
    rowb=pl.BlockSpec((L,D),lambda s,*_:(s+lo,0))
    kern,extra,alias=over_slots(attn_fwd_kernel,6,lo,before)
    b=pl.BlockSpec((8,D),lambda s,*_:(0,0))
    return pl.pallas_call(kern,
        grid_spec=pltpu.PrefetchScalarGridSpec(num_scalar_prefetch=1,grid=(hi-lo,),
            in_specs=[rowb,RESIDENT,RESIDENT,RESIDENT,b]+extra,
            out_specs=[rowb,rowb,rowb,rowb,pl.BlockSpec((L,128),lambda s,*_:(s+lo,0))]),
        input_output_aliases=alias,
        out_shape=[pltpu.HBM((R,D),BF)]*4+[pltpu.HBM((R,128),BF)],
        compiler_params=pltpu.CompilerParams(vmem_limit_bytes=30 << 20),
        cost_estimate=pl.CostEstimate(flops=2_500_000_000*(hi-lo),bytes_accessed=5_000_000*(hi-lo),transcendentals=1_700_000*(hi-lo)),
        name="attn_fwd")(lengths,*hbm(x),wq,wk,wv,sp,*before)

def attn_bwd_kernel(lo, len_ref, q_ref, k_ref, v_ref, c_ref, e_ref, g_ref, d_ref, sm_ref):
    L=q_ref.shape[0]
    s=pl.program_id(0)
    n=len_ref[s+lo]
    ln=lanes(L); even=ln<64
    row=lax.broadcasted_iota(jnp.int32,(L,128),0)
    eq=e_ref[...]
    mask=(ln==24)&(row>=n)
    zero=jnp.zeros((L,128),BF); zf=jnp.zeros((L,128),F32)
    scale=jnp.asarray(0.125,BF)
    kbase=jnp.where(mask,NEG,0.0)
    for t in range(PAIRS):
        cs=slice(128*t,128*t+128)
        q=q_ref[:,cs]; k=k_ref[:,cs]; v=v_ref[:,cs]; g=g_ref[:,cs]
        qs=q*scale
        gc=g.astype(F32)*c_ref[:,cs].astype(F32)
        ps=[];ss=[]
        for o in (0,1):
            sel=even if o==0 else ~even
            d=jnp.sum(jnp.where(sel,gc,zf),1,keepdims=True)
            dh=d.astype(BF).astype(F32); dl=d-dh
            gx=jnp.where(ln==0,-dh,jnp.where(ln==1,-dl,zf)).astype(BF)
            base=64*o+t
            hot=(ln==base)|(ln==base+8)|(ln==base+16)
            kx=jnp.where(hot,1.0,kbase).astype(BF)
            vx=jnp.where(ln<2,1.0,0.0).astype(BF)
            sc=nt(jnp.concatenate([jnp.where(sel,qs,zero),eq],1),jnp.concatenate([k,kx],1))
            p=jnp.exp(sc)
            dp=nt(jnp.concatenate([jnp.where(sel,g,zero),gx],1),jnp.concatenate([v,vx],1))
            ds=(p*dp).astype(BF)
            ps.append(p.astype(BF)); ss.append(ds)
        kk=jnp.concatenate([jnp.where(even,k,zero),jnp.where(even,zero,k)],0)
        d_ref[0,:,cs]=(mm(jnp.concatenate(ss,1),kk)*0.125).astype(BF)
        qq=jnp.concatenate([jnp.where(even,q,zero),jnp.where(even,zero,q)],0)
        gg=jnp.concatenate([jnp.where(even,g,zero),jnp.where(even,zero,g)],0)
        d_ref[1,:,cs]=(tn(jnp.concatenate(ss,0),qq)*0.125).astype(BF)
        d_ref[2,:,cs]=tn(jnp.concatenate(ps,0),gg).astype(BF)
    u=jnp.concatenate([colsum(d_ref[0].astype(F32)),colsum(d_ref[2].astype(F32)),jnp.zeros((6,D),F32)],0)
    @pl.when(s==0)
    def _(): sm_ref[...]=u
    @pl.when(s>0)
    def _(): sm_ref[...]+=u

def attn_bwd(lengths,q,k,v,c,e,g,lo,hi,before=()):
    S=lengths.shape[0]; R=q.shape[0]; L=R//S
    rowb=pl.BlockSpec((L,D),lambda s,*_:(s+lo,0))
    kern,extra,alias=over_slots(attn_bwd_kernel,7,lo,before)
    return pl.pallas_call(kern,
        grid_spec=pltpu.PrefetchScalarGridSpec(num_scalar_prefetch=1,grid=(hi-lo,),
            in_specs=[rowb,rowb,rowb,rowb,pl.BlockSpec((L,128),lambda s,*_:(s+lo,0)),rowb]+extra,
            out_specs=[pl.BlockSpec((3,L,D),lambda s,*_:(0,s+lo,0)),pl.BlockSpec((8,D),lambda s,*_:(0,0))]),
        input_output_aliases=alias,
        out_shape=[pltpu.HBM((3,R,D),BF),jax.ShapeDtypeStruct((8,D),F32)],
        compiler_params=pltpu.CompilerParams(vmem_limit_bytes=36 << 20),
        cost_estimate=pl.CostEstimate(flops=4_000_000_000*(hi-lo),bytes_accessed=6_000_000*(hi-lo),transcendentals=1_700_000*(hi-lo)),
        name="attn_bwd")(lengths,*hbm(q,k,v,c,e,g),*before)

EPS=1e-12
def gelu_parts(v):
    phi=0.5+0.5*lax.erf(v*math.sqrt(0.5))
    return v*phi, phi+v*(jnp.exp(v*v*-0.5)*(1.0/math.sqrt(2*math.pi)))
def ln_parts(h):
    mu=jnp.mean(h,1,keepdims=True); c=h-mu
    r=lax.rsqrt(jnp.mean(c*c,1,keepdims=True)+EPS)
    return c*r, r
def ln_back(up,n,r,gain):
    e=up*gain
    return r*(e-jnp.mean(e,1,keepdims=True)-n*jnp.mean(e*n,1,keepdims=True))
def colsum(x): return jnp.sum(x,0,keepdims=True)
FC=512
def once(a,b): return pl.BlockSpec((a,b),lambda s,*_:(0,0),pipeline_mode=pl.Buffered(1))
def ffn_in_kernel(x_ref,c_ref,wo_ref,we_ref,sp_ref,be_ref,n1_ref,r1_ref,fl_ref,act_ref,gp_ref):
    M=x_ref.shape[0]; FF=we_ref.shape[1]
    sp=sp_ref[...].astype(F32)
    att=mm(c_ref[...],wo_ref[...])+sp[0:1]
    n1,r1=ln_parts(x_ref[...].astype(F32)+att)
    n1_ref[...]=n1; r1_ref[...]=jnp.broadcast_to(r1,(M,128))
    fl=(n1*sp[1:2]+sp[2:3]).astype(BF); fl_ref[...]=fl
    for f in range(0,FF,FC):
        fs=slice(f,f+FC)
        a,gp=gelu_parts(mm(fl,we_ref[:,fs])+be_ref[:,fs].astype(F32))
        act_ref[:,fs]=a.astype(BF); gp_ref[:,fs]=gp.astype(BF)

def ffn_in(x,c,wo,we,sp,be,S):
    R=x.shape[0]; M=R//S; FF=we.shape[1]
    rb=lambda n:pl.BlockSpec((M,n),lambda s,*_:(s,0))
    return pl.pallas_call(ffn_in_kernel,grid=(S,),
            in_specs=[rb(D),rb(D),RESIDENT,RESIDENT,once(8,D),once(1,FF)],
            out_specs=[rb(D),rb(128),rb(D),rb(FF),rb(FF)],
        out_shape=[pltpu.HBM((R,D),F32),pltpu.HBM((R,128),F32),pltpu.HBM((R,D),BF),
            pltpu.HBM((R,FF),BF),pltpu.HBM((R,FF),BF)],
        compiler_params=pltpu.CompilerParams(vmem_limit_bytes=40 << 20),
        cost_estimate=pl.CostEstimate(flops=9_000_000_000,bytes_accessed=40_000_000,transcendentals=9_000_000),
        name="ffn_in")(*hbm(x,c),wo,we,sp,be)

def ffn_out_kernel(bk_ref,n1_ref,r1_ref,act_ref,gp_ref,go_ref,wo_ref,we_ref,ws_ref,sp_ref,
        out_ref,gs_ref,ge_ref,gr_ref,ga_ref,gc_ref,sm_ref,sb_ref):
    M=n1_ref.shape[0]; FF=we_ref.shape[1]
    s=pl.program_id(0)
    sp=sp_ref[...].astype(F32)
    bo,g1,s1,bs,g2,s2=[sp[i:i+1] for i in range(6)]
    n1=n1_ref[...]
    n2,r2=ln_parts((n1*g1+s1)+(mm(act_ref[...],ws_ref[...])+bs))
    rows=jnp.where(bk_ref[s]==0,176,jnp.where(bk_ref[s]==1,224,384))
    rm=jnp.where(lax.broadcasted_iota(jnp.int32,(M,1),0)<rows,1.0,0.0)
    out_ref[...]=((n2*g2+s2)*rm).astype(BF)
    up=go_ref[...].astype(F32)*rm
    gh=ln_back(up,n2,r2,g2)
    gs=gh.astype(BF); gs_ref[...]=gs
    acc=gh
    bsum=[]
    for f in range(0,FF,FC):
        fs=slice(f,f+FC)
        ge=(nt(gs,ws_ref[fs,:])*gp_ref[:,fs].astype(F32)).astype(BF)
        ge_ref[:,fs]=ge
        bsum.append(colsum(ge.astype(F32)))
        acc=acc+nt(ge,we_ref[:,fs])
    gr=ln_back(acc,n1,r1_ref[:,:1],g1)
    gr_ref[...]=gr
    ga=gr.astype(BF); ga_ref[...]=ga
    gc_ref[...]=nt(ga,wo_ref[...]).astype(BF)
    u=jnp.concatenate([colsum(ga.astype(F32)),colsum(acc*n1),colsum(acc),colsum(gs.astype(F32)),colsum(up*n2),colsum(up),jnp.zeros((2,D),F32)],0)
    ub=jnp.concatenate(bsum,1)
    @pl.when(s==0)
    def _():
        sm_ref[...]=u; sb_ref[...]=ub
    @pl.when(s>0)
    def _():
        sm_ref[...]+=u; sb_ref[...]+=ub

def ffn_out(buckets,n1,r1,act,gp,go,wo,we,ws,sp):
    S=buckets.shape[0]; R=n1.shape[0]; M=R//S; FF=we.shape[1]
    rb=lambda n:pl.BlockSpec((M,n),lambda s,*_:(s,0))
    full=lambda a,b:pl.BlockSpec((a,b),lambda s,*_:(0,0))
    return pl.pallas_call(ffn_out_kernel,
        grid_spec=pltpu.PrefetchScalarGridSpec(num_scalar_prefetch=1,grid=(S,),
            in_specs=[rb(D),rb(128),rb(FF),rb(FF),rb(D),RESIDENT,RESIDENT,RESIDENT,once(8,D)],
            out_specs=[rb(D),rb(D),rb(FF),rb(D),rb(D),rb(D),full(8,D),full(1,FF)]),
        out_shape=[pltpu.HBM((R,D),BF),pltpu.HBM((R,D),BF),pltpu.HBM((R,FF),BF),
            pltpu.HBM((R,D),F32),pltpu.HBM((R,D),BF),
            pltpu.HBM((R,D),BF),pltpu.HBM((8,D),F32),pltpu.HBM((1,FF),F32)],
        compiler_params=pltpu.CompilerParams(vmem_limit_bytes=48 << 20),
        cost_estimate=pl.CostEstimate(flops=24_000_000_000,bytes_accessed=60_000_000,transcendentals=0),
        name="ffn_out")(buckets,*hbm(n1,r1,act,gp,go),wo,we,ws,sp)

def tn_kernel(a_ref,b_ref,o_ref): o_ref[...]=tn(a_ref[...],b_ref[...]).astype(o_ref.dtype)
def grad_w(a,b,bm,bn,name,dt=BF,order=0):
    R,Ma=a.shape; Nb=b.shape[1]
    if order==0:
        grid=(Ma//bm,Nb//bn); ia=lambda i,j:(0,i); ib=lambda i,j:(0,j); io=lambda i,j:(i,j)
    else:
        grid=(Nb//bn,Ma//bm); ia=lambda j,i:(0,i); ib=lambda j,i:(0,j); io=lambda j,i:(i,j)
    return pl.pallas_call(tn_kernel,grid=grid,in_specs=[pl.BlockSpec((R,bm),ia),pl.BlockSpec((R,bn),ib)],
        out_specs=pl.BlockSpec((bm,bn),io),out_shape=jax.ShapeDtypeStruct((Ma,Nb),dt),
        compiler_params=pltpu.CompilerParams(vmem_limit_bytes=VM),
        cost_estimate=pl.CostEstimate(flops=2*R*Ma*Nb,bytes_accessed=2*R*(Ma+Nb)+2*Ma*Nb,transcendentals=0),
        name=name)(a,b)
def resid_kernel(gr_ref,d_ref,wa_ref,wb_ref,wc_ref,o_ref):
    o_ref[...]=gr_ref[...]+nt(d_ref[0],wa_ref[...])+nt(d_ref[1],wb_ref[...])+nt(d_ref[2],wc_ref[...])
def grad_in(gr,d,wa,wb,wc,S):
    R=gr.shape[0]; M=R//S
    rb=pl.BlockSpec((M,D),lambda s:(s,0))
    return pl.pallas_call(resid_kernel,grid=(S,),in_specs=[rb,pl.BlockSpec((3,M,D),lambda s:(0,s,0))]+[RESIDENT]*3,out_specs=rb,
        out_shape=pltpu.HBM((R,D),F32),
        compiler_params=pltpu.CompilerParams(vmem_limit_bytes=30 << 20),
        cost_estimate=pl.CostEstimate(flops=6*R*D*D,bytes_accessed=20_000_000,transcendentals=0),
        name="grad_in")(*hbm(gr,d),wa,wb,wc)

def exchange(value, pairs):
    return lax.ppermute(value, "dp", pairs)


def flip(count, mask):
    return [(i, i ^ mask) for i in range(count)]


def turn(count, even_mask, odd_mask):
    return [(i, i ^ (odd_mask if i & 1 else even_mask)) for i in range(count)]


def along_z(block):
    return jnp.stack([block] + [exchange(block, flip(32, 8 * k)) for k in (1, 2, 3)])


def near(pieces):
    return exchange(pieces, turn(32, 2, 4))


def far(pieces):
    return exchange(pieces, turn(32, 4, 2))


def both_cores(*pieces):
    return pieces + tuple(exchange(piece, flip(32, 1)) for piece in pieces)


def together(*values):
    return lax.optimization_barrier(values)


def piece_owner(me, other_core, far, near, k):
    core = me & 1
    near_mask = 2 + 2 * (core ^ other_core)
    far_mask = 6 - near_mask
    return me ^ (other_core + far * far_mask + near * near_mask + 8 * k)


def unpack_kernel(cuts, me_ref, *refs):
    pieces, outs, sems = refs[:6], refs[6:-1], refs[-1]
    me = me_ref[0]
    for other in (0, 1):
        along_z, near, far = pieces[3 * other : 3 * other + 3]
        for k in range(4):
            for ref, at, owner in (
                (along_z, k, piece_owner(me, other, 0, 0, k)),
                (near, k, piece_owner(me, other, 0, 1, k)),
                (far, k, piece_owner(me, other, 1, 0, k)),
                (far, 4 + k, piece_owner(me, other, 1, 1, k)),
            ):
                for i, start, rows, column in cuts:
                    pltpu.make_async_copy(
                        ref.at[at, pl.ds(start, rows)],
                        outs[i].at[owner, :, pl.ds(column, D)],
                        sems.at[i],
                    ).start()
    for i, out in enumerate(outs):
        pltpu.make_async_copy(out, out, sems.at[i]).wait()


def unpack(me, pieces, sizes, name):
    cuts = []
    start = 0
    for i, (rows, columns) in enumerate(sizes):
        for column in range(0, columns, D):
            cuts.append((i, start, rows, column))
            start += rows
    anywhere = pl.BlockSpec(memory_space=pl.ANY)
    return pl.pallas_call(
        functools.partial(unpack_kernel, tuple(cuts)),
        grid_spec=pltpu.PrefetchScalarGridSpec(
            num_scalar_prefetch=1,
            grid=(1,),
            in_specs=[anywhere] * 6,
            out_specs=[anywhere] * len(sizes),
            scratch_shapes=[pltpu.SemaphoreType.DMA((len(sizes),))],
        ),
        out_shape=[pltpu.VMEM((32, *size), BF) for size in sizes],
        compiler_params=pltpu.CompilerParams(vmem_limit_bytes=4 << 20),
        cost_estimate=pl.CostEstimate(
            flops=0, bytes_accessed=2 * 64 * D * start, transcendentals=0
        ),
        name=name,
    )(me, *pieces)


def place(me, total, keep, send, at):
    for other, target in ((0, keep), (1, send)):
        for far in (0, 1):
            for near in (0, 1):
                for k in range(4):
                    owner = piece_owner(me, other, far, near, k)
                    rows = total[pl.ds(pl.multiple_of(24 * owner, 8), 24), :]
                    at(target, 8 * far + 4 * near + k, rows.astype(BF))


def dw_expand_kernel(me_ref, fl_ref, ge_ref, c_ref, ga_ref, keep, send, total):
    j = pl.program_id(0)

    @pl.when(j < 4)
    def _():
        total[...] = tn(fl_ref[...], ge_ref[...])

    @pl.when(j == 4)
    def _():
        total[...] = tn(c_ref[...], ga_ref[...])

    def at(ref, piece, rows):
        ref[piece, 0] = rows

    place(me_ref[0], total, keep, send, at)


def dw_expand_packed(me, first_low, grad_expand, context, grad_attended):
    R = first_low.shape[0]
    fixed = pl.BlockSpec((R, D), lambda j, *_: (0, 0), pipeline_mode=pl.Buffered(1))
    out = pl.BlockSpec((16, 1, 24, D), lambda j, *_: (0, j, 0, 0))
    return pl.pallas_call(
        dw_expand_kernel,
        grid_spec=pltpu.PrefetchScalarGridSpec(
            num_scalar_prefetch=1,
            grid=(5,),
            in_specs=[
                fixed,
                pl.BlockSpec((R, D), lambda j, *_: (0, jnp.minimum(j, 3))),
                fixed,
                fixed,
            ],
            out_specs=[out, out],
            scratch_shapes=[pltpu.VMEM((D, D), F32)],
        ),
        out_shape=[jax.ShapeDtypeStruct((16, 5, 24, D), BF)] * 2,
        compiler_params=pltpu.CompilerParams(vmem_limit_bytes=40 << 20),
        cost_estimate=pl.CostEstimate(
            flops=10 * R * D * D, bytes_accessed=22_000_000, transcendentals=0
        ),
        name="dw_expand",
    )(me, *hbm(first_low, grad_expand, context, grad_attended))


def dw_shrink_kernel(me_ref, a_ref, gs_ref, keep, send, total):
    me = me_ref[0]
    core = me & 1
    i = pl.program_id(0)
    total[...] = tn(a_ref[...], gs_ref[...])
    for pair in range(4):
        for other, target in ((0, keep), (1, send)):
            local = 2 * pair + (core ^ other)
            away = (8 * i + local) ^ me ^ other
            side = core ^ other
            near = (away >> (1 + side)) & 1
            far = (away >> (2 - side)) & 1
            piece = 8 * far + 4 * near + (away >> 3)
            rows = total[pl.ds(pl.multiple_of(96 * local, 8), 96), :].astype(BF)
            target[piece] = rows


def dw_shrink_packed(me, active, grad_shrink):
    R = active.shape[0]
    out = pl.BlockSpec((16, 96, D), lambda i, *_: (0, 0, 0))
    return pl.pallas_call(
        dw_shrink_kernel,
        grid_spec=pltpu.PrefetchScalarGridSpec(
            num_scalar_prefetch=1,
            grid=(4,),
            in_specs=[
                pl.BlockSpec((R, D), lambda i, *_: (0, i)),
                pl.BlockSpec((R, D), lambda i, *_: (0, 0), pipeline_mode=pl.Buffered(1)),
            ],
            out_specs=[out, out],
            scratch_shapes=[pltpu.VMEM((D, D), F32)],
        ),
        out_shape=[jax.ShapeDtypeStruct((16, 96, D), BF)] * 2,
        compiler_params=pltpu.CompilerParams(vmem_limit_bytes=40 << 20),
        cost_estimate=pl.CostEstimate(
            flops=8 * R * D * D, bytes_accessed=17_000_000, transcendentals=0
        ),
        name="dw_shrink",
    )(me, *hbm(active, grad_shrink))


def dw_qkv_kernel(me_ref, x_ref, d_ref, rows_ref, keep, send, total):
    me = me_ref[0]
    i = pl.program_id(0)
    total[...] = tn(x_ref[...], d_ref[0])
    for unit in range(3):

        @pl.when(i == unit)
        def _():
            def at(ref, piece, rows):
                ref[piece, 24 * unit : 24 * unit + 24] = rows

            place(me, total, keep, send, at)

    @pl.when(i == 2)
    def _():
        for other, target in ((0, keep), (1, send)):
            for far in (0, 1):
                for near in (0, 1):
                    for k in range(4):
                        owner = piece_owner(me, other, far, near, k)
                        target[8 * far + 4 * near + k, 72:80] = rows_ref[owner]


def dw_qkv_packed(me, tokens, grads, rows):
    R = tokens.shape[0]
    out = pl.BlockSpec((16, 80, D), lambda i, *_: (0, 0, 0))
    return pl.pallas_call(
        dw_qkv_kernel,
        grid_spec=pltpu.PrefetchScalarGridSpec(
            num_scalar_prefetch=1,
            grid=(3,),
            in_specs=[
                pl.BlockSpec((R, D), lambda i, *_: (0, 0), pipeline_mode=pl.Buffered(1)),
                pl.BlockSpec((1, R, D), lambda i, *_: (i, 0, 0)),
                pl.BlockSpec((32, 8, D), lambda i, *_: (0, 0, 0)),
            ],
            out_specs=[out, out],
            scratch_shapes=[pltpu.VMEM((D, D), F32)],
        ),
        out_shape=[jax.ShapeDtypeStruct((16, 80, D), BF)] * 2,
        compiler_params=pltpu.CompilerParams(vmem_limit_bytes=30 << 20),
        cost_estimate=pl.CostEstimate(
            flops=6 * R * D * D, bytes_accessed=13_000_000, transcendentals=0
        ),
        name="dw_qkv",
    )(me, *hbm(tokens, grads), rows)


def first_kernel(*refs):
    query, key, value, *vectors, expand, out = refs
    out[0:24] = query[...]
    out[24:48] = key[...]
    out[48:72] = value[...]
    out[72:80] = jnp.zeros((8, D), BF)
    for i, vector in enumerate(vectors):
        out[72 + i : 73 + i, 0:24] = vector[...]
    out[72:73, 128:224] = expand[...]


def first_block(query, key, value, vectors, expand):
    return pl.pallas_call(
        first_kernel,
        out_shape=jax.ShapeDtypeStruct((80, D), BF),
        name="first_block",
    )(query, key, value, *[v[None] for v in vectors], expand[None])


def add_up(*parts):
    total = parts[0].astype(F32)
    for part in parts[1:]:
        total = total + part.astype(F32)
    return total


def halves(kept, came):
    n = kept.shape[0] // 2
    return (
        add_up(kept[:n], came[:n]).astype(BF),
        add_up(kept[n:], came[n:]).astype(BF),
    )


def quarters(kept, came):
    return [add_up(kept[k], came[k]).astype(BF) for k in range(4)]


def lines_of(parts):
    return [parts[0]] + [exchange(parts[k], flip(32, 8 * k)) for k in (1, 2, 3)]


def body(
    tokens,
    buckets,
    lengths,
    w_query,
    w_key,
    w_value,
    w_output,
    bias_query,
    bias_value,
    bias_output,
    gain_first,
    shift_first,
    w_expand,
    bias_expand,
    w_shrink,
    bias_shrink,
    gain_second,
    shift_second,
    grad_out,
    count,
):
    slots = buckets.shape[0]
    half = slots // 2
    whole = lambda v: lax.all_gather(v, "dp", axis=0, tiled=True)
    short = (
        bias_output,
        gain_first,
        shift_first,
        bias_shrink,
        gain_second,
        shift_second,
        bias_query,
        bias_value,
    )
    tree = count == 32
    if tree:
        me = lax.axis_index("dp").astype(jnp.int32).reshape(1)
        block_a = first_block(w_query, w_key, w_value, short, bias_expand)
        block_b = jnp.concatenate(
            [w_output] + [w_expand[:, D * i : D * i + D] for i in range(4)]
        )
        line_a = along_z(block_a)
        line_a, block_b = together(line_a, block_b)
        near_a = near(line_a)
        line_b = along_z(block_b)
        line_a, near_a, line_b, block_c = together(line_a, near_a, line_b, w_shrink)
        far_a = far(jnp.concatenate([line_a, near_a]))
        near_b = near(line_b)
        line_c = along_z(block_c)
        line_a, near_a, far_a, line_b, near_b, line_c = together(
            line_a, near_a, far_a, line_b, near_b, line_c
        )
        full_query, full_key, full_value, rows = unpack(
            me, both_cores(line_a, near_a, far_a), ((24, D),) * 3 + ((8, D),), "unpack_qkv"
        )
        full_query, full_key, full_value = [
            w.reshape(D, D) for w in (full_query, full_key, full_value)
        ]
        vectors = rows[:, :, :24].transpose(1, 0, 2).reshape(8, D)
        full_bias_expand = rows[:, 0, 128:224].reshape(1, 4 * D)
        far_b_in = jnp.concatenate([line_b, near_b])
        vectors, full_bias_expand, far_b_in, line_c = together(
            vectors, full_bias_expand, far_b_in, line_c
        )
        far_b = far(far_b_in)
        near_c = near(line_c)
        q, k, v, context, ends = attn_fwd(
            lengths, tokens, full_query, full_key, full_value, vectors, 0, slots
        )
        far_b, near_c, context = together(far_b, near_c, context)
        far_c_in = jnp.concatenate([line_c, near_c])
        full_output, full_expand = unpack(
            me, both_cores(line_b, near_b, far_b), ((24, D), (24, 4 * D)), "unpack_expand"
        )
        far_c = far(far_c_in)
        full_output = full_output.reshape(D, D)
        full_expand = full_expand.reshape(D, 4 * D)
    else:
        full_query, full_key, full_value, full_output, full_expand, full_shrink = [
            whole(w) for w in (w_query, w_key, w_value, w_output, w_expand, w_shrink)
        ]
        vectors = jnp.stack([whole(v) for v in short])
        full_bias_expand = whole(bias_expand)[None]
        q, k, v, context, ends = attn_fwd(
            lengths, tokens, full_query, full_key, full_value, vectors, 0, slots
        )

    normed, root, first_low, active, slope = ffn_in(
        tokens, context, full_output, full_expand, vectors, full_bias_expand, slots
    )
    if tree:
        far_c, normed = together(far_c, normed)
        (full_shrink,) = unpack(
            me, both_cores(line_c, near_c, far_c), ((96, D),), "unpack_shrink"
        )
        full_shrink = full_shrink.reshape(4 * D, D)
    (
        layer_out,
        grad_shrink,
        grad_expand,
        grad_h1,
        grad_attended,
        grad_context,
        sums_a,
        d_bias_expand,
    ) = ffn_out(
        buckets,
        normed,
        root,
        active,
        slope,
        grad_out,
        full_output,
        full_expand,
        full_shrink,
        vectors,
    )
    if tree:
        keep_b, send_b = dw_expand_packed(me, first_low, grad_expand, context, grad_attended)
        keep_b, send_b, active, grad_context = together(keep_b, send_b, active, grad_context)
        came_b = exchange(send_b, flip(32, 1))
        keep_c, send_c = dw_shrink_packed(me, active, grad_shrink)
        keep_c, send_c, came_b, grad_context = together(keep_c, send_c, came_b, grad_context)
        stay_b, go_b = halves(keep_b, came_b)
        stay_b, go_b, send_c, grad_context = together(stay_b, go_b, send_c, grad_context)
        came_b = far(go_b)
        came_c = exchange(send_c, flip(32, 1))
        begun, sums_b = attn_bwd(lengths, q, k, v, context, ends, grad_context, 0, half)
        sums_b, came_b, came_c = together(sums_b, came_b, came_c)
        stay_b, go_b = halves(stay_b, came_b)
        stay_c, go_c = halves(keep_c, came_c)
        grad_context, sums_b, stay_b, stay_c, go_b, go_c = together(
            grad_context, sums_b, stay_b, stay_c, go_b, go_c
        )
        came_b = near(go_b)
        came_c = far(go_c)
        grads, sums_c = attn_bwd(
            lengths, q, k, v, context, ends, grad_context, half, slots, (begun,)
        )
        sums_c, came_b, came_c = together(sums_c, came_b, came_c)
        sums_c = sums_c + sums_b
        parts_b = quarters(stay_b, came_b)
        stay_c, go_c = halves(stay_c, came_c)
        rows = jnp.concatenate([sums_a[:6], sums_c[:2]])
        rows = rows.reshape(8, 32, 24).transpose(1, 0, 2)
        long_rows = d_bias_expand.reshape(32, 1, 96)
        rows = jnp.pad(rows, ((0, 0), (0, 0), (0, D - 24))) + jnp.pad(
            long_rows, ((0, 0), (0, 7), (128, D - 224))
        )
        rows = rows.astype(BF)
        rows, stay_c, go_c, *parts_b = together(rows, stay_c, go_c, *parts_b)
        came_c = near(go_c)
        lines_b = lines_of(parts_b)
        keep_a, send_a = dw_qkv_packed(me, tokens, grads, rows)
        keep_a, send_a, came_c, *lines_b = together(keep_a, send_a, came_c, *lines_b)
        came_a = exchange(send_a, flip(32, 1))
        parts_c = quarters(stay_c, came_c)
        came_a, *parts_c = together(came_a, *parts_c)
        stay_a, go_a = halves(keep_a, came_a)
        stay_a, go_a, grad_h1, *parts_c = together(stay_a, go_a, grad_h1, *parts_c)
        came_a = far(go_a)
        lines_c = lines_of(parts_c)
    else:
        dw_expand = grad_w(first_low, grad_expand, 768, 768, "dw_expand")
        dw_output = grad_w(context, grad_attended, 768, 384, "dw_output")
        dw_shrink = grad_w(active, grad_shrink, 768, 768, "dw_shrink")
        grads, sums_c = attn_bwd(
            lengths, q, k, v, context, ends, grad_context, 0, slots
        )
        dw_query, dw_key, dw_value = [
            grad_w(tokens, grads[i], 768, 384, "dw_qkv") for i in range(3)
        ]
        sums = [sums_a[i] for i in range(6)] + [sums_c[0], sums_c[1]]
    grad_tokens = grad_in(
        grad_h1, grads, full_query, full_key, full_value, slots
    )
    if tree:
        grad_tokens, came_a, *lines_c = together(grad_tokens, came_a, *lines_c)
        stay_a, go_a = halves(stay_a, came_a)
        stay_a, go_a = together(stay_a, go_a)
        came_a = near(go_a)
        sum_b = add_up(*lines_b)
        sum_c = add_up(*lines_c)
        sum_a = add_up(*lines_of(quarters(stay_a, came_a)))
        own_query, own_key, own_value = [sum_a[24 * i : 24 * i + 24] for i in range(3)]
        own_output = sum_b[4]
        own_expand = jnp.concatenate([sum_b[i] for i in range(4)], 1)
        own_shrink = sum_c
        own_rows = sum_a[72:]
        own_short = [own_rows[i, :24] for i in range(8)]
        own_bias_expand = own_rows[0, 128:224]
    else:
        owned = lambda v: lax.psum_scatter(
            v.astype(F32), "dp", scatter_dimension=0, tiled=True
        )
        own_query, own_key, own_value, own_output, own_expand, own_shrink = [
            owned(w)
            for w in (dw_query, dw_key, dw_value, dw_output, dw_expand, dw_shrink)
        ]
        own_short = [owned(v) for v in sums]
        own_bias_expand = owned(d_bias_expand[0])
    (
        own_bias_output,
        own_gain_first,
        own_shift_first,
        own_bias_shrink,
        own_gain_second,
        own_shift_second,
        own_bias_query,
        own_bias_value,
    ) = own_short
    return (
        layer_out,
        grad_tokens,
        own_query,
        own_key,
        own_value,
        own_output,
        own_bias_query,
        own_bias_value,
        own_bias_output,
        own_gain_first,
        own_shift_first,
        own_expand,
        own_bias_expand,
        own_shrink,
        own_bias_shrink,
        own_gain_second,
        own_shift_second,
    )


def solution(mesh):
    split = P("dp")
    wide = P("dp", None)
    return jax.shard_map(
        functools.partial(body, count=mesh.shape["dp"]),
        mesh=mesh,
        in_specs=(wide, split, split)
        + (wide,) * 4
        + (split,) * 5
        + (wide, split, wide, split, split, split, wide),
        out_specs=(wide,) * 6 + (split,) * 5 + (wide, split, wide, split, split, split),
        check_vma=False,
    )
```

```python
import functools, math
import jax, jax.numpy as jnp
from jax import lax
from jax.experimental import pallas as pl
from jax.experimental.pallas import tpu as pltpu
from jax.sharding import PartitionSpec as P
BF=jnp.bfloat16; F32=jnp.float32
D=768; HD=64; PAIRS=6
VM=58<<20
NEG=-1e30
def hbm(*arrays): return [pltpu.with_memory_space_constraint(a,pltpu.HBM) for a in arrays]
def vmem(*arrays): return [pltpu.with_memory_space_constraint(a,pltpu.VMEM) for a in arrays]
RESIDENT=pl.BlockSpec(memory_space=pltpu.VMEM)
def mm(a,b): return lax.dot_general(a,b,(((1,),(0,)),((),())),preferred_element_type=F32)
def nt(a,b): return lax.dot_general(a,b,(((1,),(1,)),((),())),preferred_element_type=F32)
def tn(a,b): return lax.dot_general(a,b,(((0,),(0,)),((),())),preferred_element_type=F32)
def lanes(rows,n=128): return lax.broadcasted_iota(jnp.int32,(rows,n),1)

def attn_fwd_kernel(lo, len_ref, x_ref, wq_ref, wk_ref, wv_ref, sp_ref, q_ref, k_ref, v_ref, c_ref, e_ref):
    L=x_ref.shape[0]
    n=len_ref[pl.program_id(0)+lo]
    x=x_ref[...]
    q=(mm(x,wq_ref[...])+sp_ref[6:7].astype(F32)).astype(BF)
    k=mm(x,wk_ref[...]).astype(BF)
    v=(mm(x,wv_ref[...])+sp_ref[7:8].astype(F32)).astype(BF)
    q_ref[...]=q; k_ref[...]=k; v_ref[...]=v
    ln=lanes(L)
    even=ln<64
    row=lax.broadcasted_iota(jnp.int32,(L,128),0)
    kx=jnp.where((ln==0)&(row>=n),NEG,0.0).astype(BF)
    qx=jnp.where(ln==0,1.0,0.0).astype(BF)
    one_e=jnp.where(even,1.0,0.0).astype(BF)
    one_o=jnp.where(even,0.0,1.0).astype(BF)
    zero=jnp.zeros((L,128),BF)
    mt=jnp.zeros((L,128),F32); lt=jnp.ones((L,128),F32)
    for t in range(PAIRS):
        cs=slice(128*t,128*t+128)
        qp=q[:,cs]*jnp.asarray(0.125,BF); kp=k[:,cs]; vp=v[:,cs]
        ke=jnp.concatenate([kp,kx],1)
        ps=[];ms=[]
        for o in (0,1):
            qm=jnp.where(even if o==0 else ~even, qp, zero)
            sc=nt(jnp.concatenate([qm,qx],1),ke)
            m=jnp.max(sc,1,keepdims=True)
            ps.append(jnp.exp(sc-m).astype(BF)); ms.append(m)
        vv=jnp.concatenate([jnp.concatenate([jnp.where(even,vp,zero),one_e],1),
                            jnp.concatenate([jnp.where(even,zero,vp),one_o],1)],0)
        r=mm(jnp.concatenate(ps,1),vv)
        lb=r[:,128:]
        c_ref[:,cs]=(r[:,:128]/lb).astype(BF)
        sel_e=ln==t; sel_o=ln==64+t
        mt=jnp.where(sel_e,ms[0],jnp.where(sel_o,ms[1],mt))
        lt=jnp.where(sel_e|sel_o,lb,lt)
    neg=-(mt+jnp.log(lt))
    hi=neg.astype(BF); r1=neg-hi.astype(F32)
    mid=r1.astype(BF); rest=(r1-mid.astype(F32)).astype(BF)
    use=(ln%64)<PAIRS
    z=jnp.zeros((L,128),F32)
    e=jnp.where(use,hi.astype(F32),z)+pltpu.roll(jnp.where(use,mid.astype(F32),z),8,1)+pltpu.roll(jnp.where(use,rest.astype(F32),z),16,1)
    e=jnp.where(ln==24,1.0,e)
    e_ref[...]=e.astype(BF)

def over_slots(kernel,nin,lo,before):
    n=len(before)
    def run(*refs): kernel(lo,*refs[:nin],*refs[nin+n:])
    return run,[pl.BlockSpec(memory_space=pl.ANY)]*n,{nin+i:i for i in range(n)}

def attn_fwd(lengths,x,wq,wk,wv,sp,lo,hi,before=()):
    S=lengths.shape[0]; R=x.shape[0]; L=R//S
    rowb=pl.BlockSpec((L,D),lambda s,*_:(s+lo,0))
    kern,extra,alias=over_slots(attn_fwd_kernel,6,lo,before)
    b=pl.BlockSpec((8,D),lambda s,*_:(0,0))
    return pl.pallas_call(kern,
        grid_spec=pltpu.PrefetchScalarGridSpec(num_scalar_prefetch=1,grid=(hi-lo,),
            in_specs=[rowb,RESIDENT,RESIDENT,RESIDENT,b]+extra,
            out_specs=[rowb,rowb,rowb,rowb,pl.BlockSpec((L,128),lambda s,*_:(s+lo,0))]),
        input_output_aliases=alias,
        out_shape=[pltpu.HBM((R,D),BF)]*4+[pltpu.HBM((R,128),BF)],
        compiler_params=pltpu.CompilerParams(vmem_limit_bytes=30 << 20),
        cost_estimate=pl.CostEstimate(flops=2_500_000_000*(hi-lo),bytes_accessed=5_000_000*(hi-lo),transcendentals=1_700_000*(hi-lo)),
        name="attn_fwd")(lengths,*hbm(x),*vmem(wq,wk,wv),sp,*before)

def attn_bwd_kernel(lo, len_ref, q_ref, k_ref, v_ref, c_ref, e_ref, g_ref, d_ref, sm_ref):
    L=q_ref.shape[0]
    s=pl.program_id(0)
    n=len_ref[s+lo]
    ln=lanes(L); even=ln<64
    row=lax.broadcasted_iota(jnp.int32,(L,128),0)
    eq=e_ref[...]
    mask=(ln==24)&(row>=n)
    zero=jnp.zeros((L,128),BF); zf=jnp.zeros((L,128),F32)
    scale=jnp.asarray(0.125,BF)
    kbase=jnp.where(mask,NEG,0.0)
    for t in range(PAIRS):
        cs=slice(128*t,128*t+128)
        q=q_ref[:,cs]; k=k_ref[:,cs]; v=v_ref[:,cs]; g=g_ref[:,cs]
        qs=q*scale
        gc=g.astype(F32)*c_ref[:,cs].astype(F32)
        ps=[];ss=[]
        for o in (0,1):
            sel=even if o==0 else ~even
            d=jnp.sum(jnp.where(sel,gc,zf),1,keepdims=True)
            dh=d.astype(BF).astype(F32); dl=d-dh
            gx=jnp.where(ln==0,-dh,jnp.where(ln==1,-dl,zf)).astype(BF)
            base=64*o+t
            hot=(ln==base)|(ln==base+8)|(ln==base+16)
            kx=jnp.where(hot,1.0,kbase).astype(BF)
            vx=jnp.where(ln<2,1.0,0.0).astype(BF)
            sc=nt(jnp.concatenate([jnp.where(sel,qs,zero),eq],1),jnp.concatenate([k,kx],1))
            p=jnp.exp(sc)
            dp=nt(jnp.concatenate([jnp.where(sel,g,zero),gx],1),jnp.concatenate([v,vx],1))
            ds=(p*dp).astype(BF)
            ps.append(p.astype(BF)); ss.append(ds)
        kk=jnp.concatenate([jnp.where(even,k,zero),jnp.where(even,zero,k)],0)
        d_ref[0,:,cs]=(mm(jnp.concatenate(ss,1),kk)*0.125).astype(BF)
        qq=jnp.concatenate([jnp.where(even,q,zero),jnp.where(even,zero,q)],0)
        gg=jnp.concatenate([jnp.where(even,g,zero),jnp.where(even,zero,g)],0)
        d_ref[1,:,cs]=(tn(jnp.concatenate(ss,0),qq)*0.125).astype(BF)
        d_ref[2,:,cs]=tn(jnp.concatenate(ps,0),gg).astype(BF)
    u=jnp.concatenate([colsum(d_ref[0].astype(F32)),colsum(d_ref[2].astype(F32)),jnp.zeros((6,D),F32)],0)
    @pl.when(s==0)
    def _(): sm_ref[...]=u
    @pl.when(s>0)
    def _(): sm_ref[...]+=u

def attn_bwd(lengths,q,k,v,c,e,g,lo,hi,before=()):
    S=lengths.shape[0]; R=q.shape[0]; L=R//S
    rowb=pl.BlockSpec((L,D),lambda s,*_:(s+lo,0))
    kern,extra,alias=over_slots(attn_bwd_kernel,7,lo,before)
    return pl.pallas_call(kern,
        grid_spec=pltpu.PrefetchScalarGridSpec(num_scalar_prefetch=1,grid=(hi-lo,),
            in_specs=[rowb,rowb,rowb,rowb,pl.BlockSpec((L,128),lambda s,*_:(s+lo,0)),rowb]+extra,
            out_specs=[pl.BlockSpec((3,L,D),lambda s,*_:(0,s+lo,0)),pl.BlockSpec((8,D),lambda s,*_:(0,0))]),
        input_output_aliases=alias,
        out_shape=[pltpu.HBM((3,R,D),BF),jax.ShapeDtypeStruct((8,D),F32)],
        compiler_params=pltpu.CompilerParams(vmem_limit_bytes=36 << 20),
        cost_estimate=pl.CostEstimate(flops=4_000_000_000*(hi-lo),bytes_accessed=6_000_000*(hi-lo),transcendentals=1_700_000*(hi-lo)),
        name="attn_bwd")(lengths,*hbm(q,k,v,c,e,g),*before)

EPS=1e-12
def gelu_parts(v):
    phi=0.5+0.5*lax.erf(v*math.sqrt(0.5))
    return v*phi, phi+v*(jnp.exp(v*v*-0.5)*(1.0/math.sqrt(2*math.pi)))
def ln_parts(h):
    mu=jnp.mean(h,1,keepdims=True); c=h-mu
    r=lax.rsqrt(jnp.mean(c*c,1,keepdims=True)+EPS)
    return c*r, r
def ln_back(up,n,r,gain):
    e=up*gain
    return r*(e-jnp.mean(e,1,keepdims=True)-n*jnp.mean(e*n,1,keepdims=True))
def colsum(x): return jnp.sum(x,0,keepdims=True)
FC=512
def once(a,b): return pl.BlockSpec((a,b),lambda s,*_:(0,0),pipeline_mode=pl.Buffered(1))
def ffn_in_kernel(x_ref,c_ref,wo_ref,we_ref,sp_ref,be_ref,n1_ref,r1_ref,fl_ref,act_ref,gp_ref):
    M=x_ref.shape[0]; FF=we_ref.shape[1]
    sp=sp_ref[...].astype(F32)
    att=mm(c_ref[...],wo_ref[...])+sp[0:1]
    n1,r1=ln_parts(x_ref[...].astype(F32)+att)
    n1_ref[...]=n1; r1_ref[...]=jnp.broadcast_to(r1,(M,128))
    fl=(n1*sp[1:2]+sp[2:3]).astype(BF); fl_ref[...]=fl
    for f in range(0,FF,FC):
        fs=slice(f,f+FC)
        a,gp=gelu_parts(mm(fl,we_ref[:,fs])+be_ref[:,fs].astype(F32))
        act_ref[:,fs]=a.astype(BF); gp_ref[:,fs]=gp.astype(BF)

def ffn_in(x,c,wo,we,sp,be,S):
    R=x.shape[0]; M=R//S; FF=we.shape[1]
    rb=lambda n:pl.BlockSpec((M,n),lambda s,*_:(s,0))
    return pl.pallas_call(ffn_in_kernel,grid=(S,),
            in_specs=[rb(D),rb(D),RESIDENT,RESIDENT,once(8,D),once(1,FF)],
            out_specs=[rb(D),rb(128),rb(D),rb(FF),rb(FF)],
        out_shape=[pltpu.HBM((R,D),F32),pltpu.HBM((R,128),F32),pltpu.HBM((R,D),BF),
            pltpu.HBM((R,FF),BF),pltpu.HBM((R,FF),BF)],
        compiler_params=pltpu.CompilerParams(vmem_limit_bytes=40 << 20),
        cost_estimate=pl.CostEstimate(flops=9_000_000_000,bytes_accessed=40_000_000,transcendentals=9_000_000),
        name="ffn_in")(*hbm(x,c),*vmem(wo,we),sp,be)

def ffn_out_kernel(bk_ref,n1_ref,r1_ref,act_ref,gp_ref,go_ref,wo_ref,we_ref,ws_ref,sp_ref,
        out_ref,gs_ref,ge_ref,gr_ref,ga_ref,gc_ref,sm_ref,sb_ref):
    M=n1_ref.shape[0]; FF=we_ref.shape[1]
    s=pl.program_id(0)
    sp=sp_ref[...].astype(F32)
    bo,g1,s1,bs,g2,s2=[sp[i:i+1] for i in range(6)]
    n1=n1_ref[...]
    n2,r2=ln_parts((n1*g1+s1)+(mm(act_ref[...],ws_ref[...])+bs))
    rows=jnp.where(bk_ref[s]==0,176,jnp.where(bk_ref[s]==1,224,384))
    rm=jnp.where(lax.broadcasted_iota(jnp.int32,(M,1),0)<rows,1.0,0.0)
    out_ref[...]=((n2*g2+s2)*rm).astype(BF)
    up=go_ref[...].astype(F32)*rm
    gh=ln_back(up,n2,r2,g2)
    gs=gh.astype(BF); gs_ref[...]=gs
    acc=gh
    bsum=[]
    for f in range(0,FF,FC):
        fs=slice(f,f+FC)
        ge=(nt(gs,ws_ref[fs,:])*gp_ref[:,fs].astype(F32)).astype(BF)
        ge_ref[:,fs]=ge
        bsum.append(colsum(ge.astype(F32)))
        acc=acc+nt(ge,we_ref[:,fs])
    gr=ln_back(acc,n1,r1_ref[:,:1],g1)
    gr_ref[...]=gr
    ga=gr.astype(BF); ga_ref[...]=ga
    gc_ref[...]=nt(ga,wo_ref[...]).astype(BF)
    u=jnp.concatenate([colsum(ga.astype(F32)),colsum(acc*n1),colsum(acc),colsum(gs.astype(F32)),colsum(up*n2),colsum(up),jnp.zeros((2,D),F32)],0)
    ub=jnp.concatenate(bsum,1)
    @pl.when(s==0)
    def _():
        sm_ref[...]=u; sb_ref[...]=ub
    @pl.when(s>0)
    def _():
        sm_ref[...]+=u; sb_ref[...]+=ub

def ffn_out(buckets,n1,r1,act,gp,go,wo,we,ws,sp):
    S=buckets.shape[0]; R=n1.shape[0]; M=R//S; FF=we.shape[1]
    rb=lambda n:pl.BlockSpec((M,n),lambda s,*_:(s,0))
    full=lambda a,b:pl.BlockSpec((a,b),lambda s,*_:(0,0))
    return pl.pallas_call(ffn_out_kernel,
        grid_spec=pltpu.PrefetchScalarGridSpec(num_scalar_prefetch=1,grid=(S,),
            in_specs=[rb(D),rb(128),rb(FF),rb(FF),rb(D),RESIDENT,RESIDENT,RESIDENT,once(8,D)],
            out_specs=[rb(D),rb(D),rb(FF),rb(D),rb(D),rb(D),full(8,D),full(1,FF)]),
        out_shape=[pltpu.HBM((R,D),BF),pltpu.HBM((R,D),BF),pltpu.HBM((R,FF),BF),
            pltpu.HBM((R,D),F32),pltpu.HBM((R,D),BF),
            pltpu.HBM((R,D),BF),pltpu.HBM((8,D),F32),pltpu.HBM((1,FF),F32)],
        compiler_params=pltpu.CompilerParams(vmem_limit_bytes=48 << 20),
        cost_estimate=pl.CostEstimate(flops=24_000_000_000,bytes_accessed=60_000_000,transcendentals=0),
        name="ffn_out")(buckets,*hbm(n1,r1,act,gp,go),*vmem(wo,we,ws),sp)

def tn_kernel(a_ref,b_ref,o_ref): o_ref[...]=tn(a_ref[...],b_ref[...]).astype(o_ref.dtype)
def grad_w(a,b,bm,bn,name,dt=BF,order=0):
    R,Ma=a.shape; Nb=b.shape[1]
    if order==0:
        grid=(Ma//bm,Nb//bn); ia=lambda i,j:(0,i); ib=lambda i,j:(0,j); io=lambda i,j:(i,j)
    else:
        grid=(Nb//bn,Ma//bm); ia=lambda j,i:(0,i); ib=lambda j,i:(0,j); io=lambda j,i:(i,j)
    return pl.pallas_call(tn_kernel,grid=grid,in_specs=[pl.BlockSpec((R,bm),ia),pl.BlockSpec((R,bn),ib)],
        out_specs=pl.BlockSpec((bm,bn),io),out_shape=jax.ShapeDtypeStruct((Ma,Nb),dt),
        compiler_params=pltpu.CompilerParams(vmem_limit_bytes=VM),
        cost_estimate=pl.CostEstimate(flops=2*R*Ma*Nb,bytes_accessed=2*R*(Ma+Nb)+2*Ma*Nb,transcendentals=0),
        name=name)(a,b)
def resid_kernel(gr_ref,d_ref,wa_ref,wb_ref,wc_ref,o_ref):
    o_ref[...]=gr_ref[...]+nt(d_ref[0],wa_ref[...])+nt(d_ref[1],wb_ref[...])+nt(d_ref[2],wc_ref[...])
def grad_in(gr,d,wa,wb,wc,S):
    R=gr.shape[0]; M=R//S
    rb=pl.BlockSpec((M,D),lambda s:(s,0))
    return pl.pallas_call(resid_kernel,grid=(S,),in_specs=[rb,pl.BlockSpec((3,M,D),lambda s:(0,s,0))]+[RESIDENT]*3,out_specs=rb,
        out_shape=pltpu.HBM((R,D),F32),
        compiler_params=pltpu.CompilerParams(vmem_limit_bytes=30 << 20),
        cost_estimate=pl.CostEstimate(flops=6*R*D*D,bytes_accessed=20_000_000,transcendentals=0),
        name="grad_in")(*hbm(gr,d),wa,wb,wc)

def exchange(value, pairs):
    return lax.ppermute(value, "dp", pairs)


def flip(count, mask):
    return [(i, i ^ mask) for i in range(count)]


def turn(count, even_mask, odd_mask):
    return [(i, i ^ (odd_mask if i & 1 else even_mask)) for i in range(count)]


def along_z(block):
    return jnp.stack([block] + [exchange(block, flip(32, 8 * k)) for k in (1, 2, 3)])


def near(pieces):
    return exchange(pieces, turn(32, 2, 4))


def far(pieces):
    return exchange(pieces, turn(32, 4, 2))


def both_cores(*pieces):
    return pieces + tuple(exchange(piece, flip(32, 1)) for piece in pieces)


def together(*values):
    return lax.optimization_barrier(values)


def piece_owner(me, other_core, far, near, k):
    core = me & 1
    near_mask = 2 + 2 * (core ^ other_core)
    far_mask = 6 - near_mask
    return me ^ (other_core + far * far_mask + near * near_mask + 8 * k)


def unpack_kernel(cuts, me_ref, *refs):
    pieces, outs, sems = refs[:6], refs[6:-1], refs[-1]
    me = me_ref[0]
    for other in (0, 1):
        along_z, near, far = pieces[3 * other : 3 * other + 3]
        for k in range(4):
            for ref, at, owner in (
                (along_z, k, piece_owner(me, other, 0, 0, k)),
                (near, k, piece_owner(me, other, 0, 1, k)),
                (far, k, piece_owner(me, other, 1, 0, k)),
                (far, 4 + k, piece_owner(me, other, 1, 1, k)),
            ):
                for i, start, rows, column in cuts:
                    pltpu.make_async_copy(
                        ref.at[at, pl.ds(start, rows)],
                        outs[i].at[owner, :, pl.ds(column, D)],
                        sems.at[i],
                    ).start()
    for i, out in enumerate(outs):
        pltpu.make_async_copy(out, out, sems.at[i]).wait()


def unpack(me, pieces, sizes, name):
    cuts = []
    start = 0
    for i, (rows, columns) in enumerate(sizes):
        for column in range(0, columns, D):
            cuts.append((i, start, rows, column))
            start += rows
    anywhere = pl.BlockSpec(memory_space=pl.ANY)
    return pl.pallas_call(
        functools.partial(unpack_kernel, tuple(cuts)),
        grid_spec=pltpu.PrefetchScalarGridSpec(
            num_scalar_prefetch=1,
            grid=(1,),
            in_specs=[anywhere] * 6,
            out_specs=[anywhere] * len(sizes),
            scratch_shapes=[pltpu.SemaphoreType.DMA((len(sizes),))],
        ),
        out_shape=[pltpu.VMEM((32, *size), BF) for size in sizes],
        compiler_params=pltpu.CompilerParams(vmem_limit_bytes=4 << 20),
        cost_estimate=pl.CostEstimate(
            flops=0, bytes_accessed=2 * 64 * D * start, transcendentals=0
        ),
        name=name,
    )(me, *pieces)


def place(me, total, keep, send, at):
    for other, target in ((0, keep), (1, send)):
        for far in (0, 1):
            for near in (0, 1):
                for k in range(4):
                    owner = piece_owner(me, other, far, near, k)
                    rows = total[pl.ds(pl.multiple_of(24 * owner, 8), 24), :]
                    at(target, 8 * far + 4 * near + k, rows.astype(BF))


def dw_expand_kernel(me_ref, fl_ref, ge_ref, c_ref, ga_ref, keep, send, total):
    j = pl.program_id(0)

    @pl.when(j < 4)
    def _():
        total[...] = tn(fl_ref[...], ge_ref[...])

    @pl.when(j == 4)
    def _():
        total[...] = tn(c_ref[...], ga_ref[...])

    def at(ref, piece, rows):
        ref[piece, 0] = rows

    place(me_ref[0], total, keep, send, at)


def dw_expand_packed(me, first_low, grad_expand, context, grad_attended):
    R = first_low.shape[0]
    fixed = pl.BlockSpec((R, D), lambda j, *_: (0, 0), pipeline_mode=pl.Buffered(1))
    out = pl.BlockSpec((16, 1, 24, D), lambda j, *_: (0, j, 0, 0))
    return pl.pallas_call(
        dw_expand_kernel,
        grid_spec=pltpu.PrefetchScalarGridSpec(
            num_scalar_prefetch=1,
            grid=(5,),
            in_specs=[
                fixed,
                pl.BlockSpec((R, D), lambda j, *_: (0, jnp.minimum(j, 3))),
                fixed,
                fixed,
            ],
            out_specs=[out, out],
            scratch_shapes=[pltpu.VMEM((D, D), F32)],
        ),
        out_shape=[jax.ShapeDtypeStruct((16, 5, 24, D), BF)] * 2,
        compiler_params=pltpu.CompilerParams(vmem_limit_bytes=40 << 20),
        cost_estimate=pl.CostEstimate(
            flops=10 * R * D * D, bytes_accessed=22_000_000, transcendentals=0
        ),
        name="dw_expand",
    )(me, *hbm(first_low, grad_expand, context, grad_attended))


def dw_shrink_kernel(me_ref, a_ref, gs_ref, keep, send, total):
    me = me_ref[0]
    core = me & 1
    i = pl.program_id(0)
    total[...] = tn(a_ref[...], gs_ref[...])
    for pair in range(4):
        for other, target in ((0, keep), (1, send)):
            local = 2 * pair + (core ^ other)
            away = (8 * i + local) ^ me ^ other
            side = core ^ other
            near = (away >> (1 + side)) & 1
            far = (away >> (2 - side)) & 1
            piece = 8 * far + 4 * near + (away >> 3)
            rows = total[pl.ds(pl.multiple_of(96 * local, 8), 96), :].astype(BF)
            target[piece] = rows


def dw_shrink_packed(me, active, grad_shrink):
    R = active.shape[0]
    out = pl.BlockSpec((16, 96, D), lambda i, *_: (0, 0, 0))
    return pl.pallas_call(
        dw_shrink_kernel,
        grid_spec=pltpu.PrefetchScalarGridSpec(
            num_scalar_prefetch=1,
            grid=(4,),
            in_specs=[
                pl.BlockSpec((R, D), lambda i, *_: (0, i)),
                pl.BlockSpec((R, D), lambda i, *_: (0, 0), pipeline_mode=pl.Buffered(1)),
            ],
            out_specs=[out, out],
            scratch_shapes=[pltpu.VMEM((D, D), F32)],
        ),
        out_shape=[jax.ShapeDtypeStruct((16, 96, D), BF)] * 2,
        compiler_params=pltpu.CompilerParams(vmem_limit_bytes=40 << 20),
        cost_estimate=pl.CostEstimate(
            flops=8 * R * D * D, bytes_accessed=17_000_000, transcendentals=0
        ),
        name="dw_shrink",
    )(me, *hbm(active, grad_shrink))


def dw_qkv_kernel(me_ref, x_ref, d_ref, rows_ref, keep, send, total):
    me = me_ref[0]
    i = pl.program_id(0)
    total[...] = tn(x_ref[...], d_ref[0])
    for unit in range(3):

        @pl.when(i == unit)
        def _():
            def at(ref, piece, rows):
                ref[piece, 24 * unit : 24 * unit + 24] = rows

            place(me, total, keep, send, at)

    @pl.when(i == 2)
    def _():
        for other, target in ((0, keep), (1, send)):
            for far in (0, 1):
                for near in (0, 1):
                    for k in range(4):
                        owner = piece_owner(me, other, far, near, k)
                        target[8 * far + 4 * near + k, 72:80] = rows_ref[owner]


def dw_qkv_packed(me, tokens, grads, rows):
    R = tokens.shape[0]
    out = pl.BlockSpec((16, 80, D), lambda i, *_: (0, 0, 0))
    return pl.pallas_call(
        dw_qkv_kernel,
        grid_spec=pltpu.PrefetchScalarGridSpec(
            num_scalar_prefetch=1,
            grid=(3,),
            in_specs=[
                pl.BlockSpec((R, D), lambda i, *_: (0, 0), pipeline_mode=pl.Buffered(1)),
                pl.BlockSpec((1, R, D), lambda i, *_: (i, 0, 0)),
                pl.BlockSpec((32, 8, D), lambda i, *_: (0, 0, 0)),
            ],
            out_specs=[out, out],
            scratch_shapes=[pltpu.VMEM((D, D), F32)],
        ),
        out_shape=[jax.ShapeDtypeStruct((16, 80, D), BF)] * 2,
        compiler_params=pltpu.CompilerParams(vmem_limit_bytes=30 << 20),
        cost_estimate=pl.CostEstimate(
            flops=6 * R * D * D, bytes_accessed=13_000_000, transcendentals=0
        ),
        name="dw_qkv",
    )(me, *hbm(tokens, grads), rows)


def first_kernel(*refs):
    query, key, value, *vectors, expand, out = refs
    out[0:24] = query[...]
    out[24:48] = key[...]
    out[48:72] = value[...]
    out[72:80] = jnp.zeros((8, D), BF)
    for i, vector in enumerate(vectors):
        out[72 + i : 73 + i, 0:24] = vector[...]
    out[72:73, 128:224] = expand[...]


def first_block(query, key, value, vectors, expand):
    return pl.pallas_call(
        first_kernel,
        out_shape=jax.ShapeDtypeStruct((80, D), BF),
        name="first_block",
    )(query, key, value, *[v[None] for v in vectors], expand[None])


def add_up(*parts):
    total = parts[0].astype(F32)
    for part in parts[1:]:
        total = total + part.astype(F32)
    return total


def halves(kept, came):
    n = kept.shape[0] // 2
    return (
        add_up(kept[:n], came[:n]).astype(BF),
        add_up(kept[n:], came[n:]).astype(BF),
    )


def quarters(kept, came):
    return [add_up(kept[k], came[k]).astype(BF) for k in range(4)]


def lines_of(parts):
    return [parts[0]] + [exchange(parts[k], flip(32, 8 * k)) for k in (1, 2, 3)]


def body(
    tokens,
    buckets,
    lengths,
    w_query,
    w_key,
    w_value,
    w_output,
    bias_query,
    bias_value,
    bias_output,
    gain_first,
    shift_first,
    w_expand,
    bias_expand,
    w_shrink,
    bias_shrink,
    gain_second,
    shift_second,
    grad_out,
    count,
):
    slots = buckets.shape[0]
    half = slots // 2
    whole = lambda v: lax.all_gather(v, "dp", axis=0, tiled=True)
    short = (
        bias_output,
        gain_first,
        shift_first,
        bias_shrink,
        gain_second,
        shift_second,
        bias_query,
        bias_value,
    )
    tree = count == 32
    if tree:
        me = lax.axis_index("dp").astype(jnp.int32).reshape(1)
        block_a = first_block(w_query, w_key, w_value, short, bias_expand)
        block_b = jnp.concatenate(
            [w_output] + [w_expand[:, D * i : D * i + D] for i in range(4)]
        )
        line_a = along_z(block_a)
        line_a, block_b = together(line_a, block_b)
        near_a = near(line_a)
        line_b = along_z(block_b)
        line_a, near_a, line_b, block_c = together(line_a, near_a, line_b, w_shrink)
        far_a = far(jnp.concatenate([line_a, near_a]))
        near_b = near(line_b)
        line_c = along_z(block_c)
        line_a, near_a, far_a, line_b, near_b, line_c = together(
            line_a, near_a, far_a, line_b, near_b, line_c
        )
        full_query, full_key, full_value, rows = unpack(
            me, both_cores(line_a, near_a, far_a), ((24, D),) * 3 + ((8, D),), "unpack_qkv"
        )
        full_query, full_key, full_value = [
            w.reshape(D, D) for w in (full_query, full_key, full_value)
        ]
        vectors = rows[:, :, :24].transpose(1, 0, 2).reshape(8, D)
        full_bias_expand = rows[:, 0, 128:224].reshape(1, 4 * D)
        far_b_in = jnp.concatenate([line_b, near_b])
        vectors, full_bias_expand, far_b_in, line_c = together(
            vectors, full_bias_expand, far_b_in, line_c
        )
        far_b = far(far_b_in)
        near_c = near(line_c)
        q, k, v, context, ends = attn_fwd(
            lengths, tokens, full_query, full_key, full_value, vectors, 0, slots
        )
        far_b, near_c, context = together(far_b, near_c, context)
        far_c_in = jnp.concatenate([line_c, near_c])
        full_output, full_expand = unpack(
            me, both_cores(line_b, near_b, far_b), ((24, D), (24, 4 * D)), "unpack_expand"
        )
        far_c = far(far_c_in)
        full_output = full_output.reshape(D, D)
        full_expand = full_expand.reshape(D, 4 * D)
    else:
        full_query, full_key, full_value, full_output, full_expand, full_shrink = [
            whole(w) for w in (w_query, w_key, w_value, w_output, w_expand, w_shrink)
        ]
        vectors = jnp.stack([whole(v) for v in short])
        full_bias_expand = whole(bias_expand)[None]
        q, k, v, context, ends = attn_fwd(
            lengths, tokens, full_query, full_key, full_value, vectors, 0, slots
        )

    normed, root, first_low, active, slope = ffn_in(
        tokens, context, full_output, full_expand, vectors, full_bias_expand, slots
    )
    if tree:
        far_c, normed = together(far_c, normed)
        (full_shrink,) = unpack(
            me, both_cores(line_c, near_c, far_c), ((96, D),), "unpack_shrink"
        )
        full_shrink = full_shrink.reshape(4 * D, D)
    (
        layer_out,
        grad_shrink,
        grad_expand,
        grad_h1,
        grad_attended,
        grad_context,
        sums_a,
        d_bias_expand,
    ) = ffn_out(
        buckets,
        normed,
        root,
        active,
        slope,
        grad_out,
        full_output,
        full_expand,
        full_shrink,
        vectors,
    )
    if tree:
        keep_b, send_b = dw_expand_packed(me, first_low, grad_expand, context, grad_attended)
        keep_b, send_b, active, grad_context = together(keep_b, send_b, active, grad_context)
        came_b = exchange(send_b, flip(32, 1))
        keep_c, send_c = dw_shrink_packed(me, active, grad_shrink)
        keep_c, send_c, came_b, grad_context = together(keep_c, send_c, came_b, grad_context)
        stay_b, go_b = halves(keep_b, came_b)
        stay_b, go_b, send_c, grad_context = together(stay_b, go_b, send_c, grad_context)
        came_b = far(go_b)
        came_c = exchange(send_c, flip(32, 1))
        begun, sums_b = attn_bwd(lengths, q, k, v, context, ends, grad_context, 0, half)
        sums_b, came_b, came_c = together(sums_b, came_b, came_c)
        stay_b, go_b = halves(stay_b, came_b)
        stay_c, go_c = halves(keep_c, came_c)
        grad_context, sums_b, stay_b, stay_c, go_b, go_c = together(
            grad_context, sums_b, stay_b, stay_c, go_b, go_c
        )
        came_b = near(go_b)
        came_c = far(go_c)
        grads, sums_c = attn_bwd(
            lengths, q, k, v, context, ends, grad_context, half, slots, (begun,)
        )
        sums_c, came_b, came_c = together(sums_c, came_b, came_c)
        sums_c = sums_c + sums_b
        parts_b = quarters(stay_b, came_b)
        stay_c, go_c = halves(stay_c, came_c)
        rows = jnp.concatenate([sums_a[:6], sums_c[:2]])
        rows = rows.reshape(8, 32, 24).transpose(1, 0, 2)
        long_rows = d_bias_expand.reshape(32, 1, 96)
        rows = jnp.pad(rows, ((0, 0), (0, 0), (0, D - 24))) + jnp.pad(
            long_rows, ((0, 0), (0, 7), (128, D - 224))
        )
        rows = rows.astype(BF)
        rows, stay_c, go_c, *parts_b = together(rows, stay_c, go_c, *parts_b)
        came_c = near(go_c)
        lines_b = lines_of(parts_b)
        keep_a, send_a = dw_qkv_packed(me, tokens, grads, rows)
        keep_a, send_a, came_c, *lines_b = together(keep_a, send_a, came_c, *lines_b)
        came_a = exchange(send_a, flip(32, 1))
        parts_c = quarters(stay_c, came_c)
        came_a, *parts_c = together(came_a, *parts_c)
        stay_a, go_a = halves(keep_a, came_a)
        stay_a, go_a, grad_h1, *parts_c = together(stay_a, go_a, grad_h1, *parts_c)
        came_a = far(go_a)
        lines_c = lines_of(parts_c)
    else:
        dw_expand = grad_w(first_low, grad_expand, 768, 768, "dw_expand")
        dw_output = grad_w(context, grad_attended, 768, 384, "dw_output")
        dw_shrink = grad_w(active, grad_shrink, 768, 768, "dw_shrink")
        grads, sums_c = attn_bwd(
            lengths, q, k, v, context, ends, grad_context, 0, slots
        )
        dw_query, dw_key, dw_value = [
            grad_w(tokens, grads[i], 768, 384, "dw_qkv") for i in range(3)
        ]
        sums = [sums_a[i] for i in range(6)] + [sums_c[0], sums_c[1]]
    grad_tokens = grad_in(
        grad_h1, grads, full_query, full_key, full_value, slots
    )
    if tree:
        grad_tokens, came_a, *lines_c = together(grad_tokens, came_a, *lines_c)
        stay_a, go_a = halves(stay_a, came_a)
        stay_a, go_a = together(stay_a, go_a)
        came_a = near(go_a)
        sum_b = add_up(*lines_b)
        sum_c = add_up(*lines_c)
        sum_a = add_up(*lines_of(quarters(stay_a, came_a)))
        own_query, own_key, own_value = [sum_a[24 * i : 24 * i + 24] for i in range(3)]
        own_output = sum_b[4]
        own_expand = jnp.concatenate([sum_b[i] for i in range(4)], 1)
        own_shrink = sum_c
        own_rows = sum_a[72:]
        own_short = [own_rows[i, :24] for i in range(8)]
        own_bias_expand = own_rows[0, 128:224]
    else:
        owned = lambda v: lax.psum_scatter(
            v.astype(F32), "dp", scatter_dimension=0, tiled=True
        )
        own_query, own_key, own_value, own_output, own_expand, own_shrink = [
            owned(w)
            for w in (dw_query, dw_key, dw_value, dw_output, dw_expand, dw_shrink)
        ]
        own_short = [owned(v) for v in sums]
        own_bias_expand = owned(d_bias_expand[0])
    (
        own_bias_output,
        own_gain_first,
        own_shift_first,
        own_bias_shrink,
        own_gain_second,
        own_shift_second,
        own_bias_query,
        own_bias_value,
    ) = own_short
    return (
        layer_out,
        grad_tokens,
        own_query,
        own_key,
        own_value,
        own_output,
        own_bias_query,
        own_bias_value,
        own_bias_output,
        own_gain_first,
        own_shift_first,
        own_expand,
        own_bias_expand,
        own_shrink,
        own_bias_shrink,
        own_gain_second,
        own_shift_second,
    )


def solution(mesh):
    split = P("dp")
    wide = P("dp", None)
    return jax.shard_map(
        functools.partial(body, count=mesh.shape["dp"]),
        mesh=mesh,
        in_specs=(wide, split, split)
        + (wide,) * 4
        + (split,) * 5
        + (wide, split, wide, split, split, split, wide),
        out_specs=(wide,) * 6 + (split,) * 5 + (wide, split, wide, split, split, split),
        check_vma=False,
    )
```

```python
import functools, math
import jax, jax.numpy as jnp
from jax import lax
from jax.experimental import pallas as pl
from jax.experimental.pallas import tpu as pltpu
from jax.sharding import PartitionSpec as P
BF=jnp.bfloat16; F32=jnp.float32
D=768; HD=64; PAIRS=3
W3=1152
WP=1280
EPS=1e-12
VM=58<<20
NEG=-1e30
def hbm(*arrays): return [pltpu.with_memory_space_constraint(a,pltpu.HBM) for a in arrays]
def vmem(*arrays): return [pltpu.with_memory_space_constraint(a,pltpu.VMEM) for a in arrays]
RESIDENT=pl.BlockSpec(memory_space=pltpu.VMEM)
def mm(a,b): return lax.dot_general(a,b,(((1,),(0,)),((),())),preferred_element_type=F32)
def nt(a,b): return lax.dot_general(a,b,(((1,),(1,)),((),())),preferred_element_type=F32)
def tn(a,b): return lax.dot_general(a,b,(((0,),(0,)),((),())),preferred_element_type=F32)
def lanes(rows,n=128): return lax.broadcasted_iota(jnp.int32,(rows,n),1)

def attn_fwd_kernel(side, len_ref, x_ref, w_ref, sp_ref, *refs):
    f_ref,c_ref,e_ref=refs[-3:]
    L=x_ref.shape[0]
    n=len_ref[pl.program_id(0)]
    x=x_ref[...]
    f=mm(x,w_ref[:,:W3])
    cut=384*side
    q=(f[:,:384]+sp_ref[6:7,cut:cut+384].astype(F32)).astype(BF)
    k=f[:,384:768].astype(BF)
    v=(f[:,768:]+sp_ref[7:8,cut:cut+384].astype(F32)).astype(BF)
    f_ref[:,:384]=q; f_ref[:,384:768]=k; f_ref[:,768:]=v
    ln=lanes(L)
    even=ln<64
    row=lax.broadcasted_iota(jnp.int32,(L,128),0)
    kx=jnp.where((ln==0)&(row>=n),NEG,0.0).astype(BF)
    qx=jnp.where(ln==0,1.0,0.0).astype(BF)
    one_e=jnp.where(even,1.0,0.0).astype(BF)
    one_o=jnp.where(even,0.0,1.0).astype(BF)
    zero=jnp.zeros((L,128),BF)
    mt=jnp.zeros((L,128),F32); lt=jnp.ones((L,128),F32)
    for t in range(PAIRS):
        cs=slice(128*t,128*t+128)
        qp=q[:,cs]*jnp.asarray(0.125,BF); kp=k[:,cs]; vp=v[:,cs]
        ke=jnp.concatenate([kp,kx],1)
        ps=[];ms=[]
        for o in (0,1):
            qm=jnp.where(even if o==0 else ~even, qp, zero)
            sc=nt(jnp.concatenate([qm,qx],1),ke)
            m=jnp.max(sc,1,keepdims=True)
            ps.append(jnp.exp(sc-m).astype(BF)); ms.append(m)
        vv=jnp.concatenate([jnp.concatenate([jnp.where(even,vp,zero),one_e],1),
                            jnp.concatenate([jnp.where(even,zero,vp),one_o],1)],0)
        r=mm(jnp.concatenate(ps,1),vv)
        lb=r[:,128:]
        c_ref[:,cs]=(r[:,:128]/lb).astype(BF)
        sel_e=ln==t; sel_o=ln==64+t
        mt=jnp.where(sel_e,ms[0],jnp.where(sel_o,ms[1],mt))
        lt=jnp.where(sel_e|sel_o,lb,lt)
    neg=-(mt+jnp.log(lt))
    hi=neg.astype(BF); r1=neg-hi.astype(F32)
    mid=r1.astype(BF); rest=(r1-mid.astype(F32)).astype(BF)
    use=(ln%64)<PAIRS
    z=jnp.zeros((L,128),F32)
    e=jnp.where(use,hi.astype(F32),z)+pltpu.roll(jnp.where(use,mid.astype(F32),z),8,1)+pltpu.roll(jnp.where(use,rest.astype(F32),z),16,1)
    e=jnp.where(ln==24,1.0,e)
    e_ref[...]=e.astype(BF)

def attn_fwd(side,lengths,x,w,sp,*begun):
    S=lengths.shape[0]; R=x.shape[0]; L=R//S
    rb=lambda n:pl.BlockSpec((L,n),lambda s,*_:(s,0))
    return pl.pallas_call(functools.partial(attn_fwd_kernel,side),input_output_aliases={4:1} if begun else {},
        grid_spec=pltpu.PrefetchScalarGridSpec(num_scalar_prefetch=1,grid=(S,),
            in_specs=[rb(D),RESIDENT,pl.BlockSpec((8,D),lambda s,*_:(0,0))]+[pl.BlockSpec(memory_space=pl.ANY)]*len(begun),
            out_specs=[rb(W3),pl.BlockSpec((L,384),lambda s,*_:(s,side)),rb(128)]),
        out_shape=[pltpu.HBM((R,W3),BF),pltpu.HBM((R,D),BF),pltpu.HBM((R,128),BF)],
        compiler_params=pltpu.CompilerParams(vmem_limit_bytes=36<<20),
        cost_estimate=pl.CostEstimate(flops=5_000_000_000,bytes_accessed=10_000_000,transcendentals=3_500_000),
        name="attn_fwd")(lengths,*hbm(x),*vmem(w),sp,*begun)

def attn_bwd_kernel(len_ref, f_ref, c_ref, e_ref, g_ref, d_ref, sm_ref):
    L=f_ref.shape[0]
    s=pl.program_id(0)
    n=len_ref[s]
    ln=lanes(L); even=ln<64
    row=lax.broadcasted_iota(jnp.int32,(L,128),0)
    eq=e_ref[...]
    mask=(ln==24)&(row>=n)
    zero=jnp.zeros((L,128),BF); zf=jnp.zeros((L,128),F32)
    scale=jnp.asarray(0.125,BF)
    kbase=jnp.where(mask,NEG,0.0)
    for t in range(PAIRS):
        cs=slice(128*t,128*t+128)
        ck=slice(384+128*t,512+128*t); cv=slice(768+128*t,896+128*t)
        q=f_ref[:,cs]; k=f_ref[:,ck]; v=f_ref[:,cv]; g=g_ref[:,cs]
        qs=q*scale
        gc=g.astype(F32)*c_ref[:,cs].astype(F32)
        ps=[];ss=[]
        for o in (0,1):
            sel=even if o==0 else ~even
            d=jnp.sum(jnp.where(sel,gc,zf),1,keepdims=True)
            dh=d.astype(BF).astype(F32); dl=d-dh
            gx=jnp.where(ln==0,-dh,jnp.where(ln==1,-dl,zf)).astype(BF)
            base=64*o+t
            hot=(ln==base)|(ln==base+8)|(ln==base+16)
            kx=jnp.where(hot,1.0,kbase).astype(BF)
            vx=jnp.where(ln<2,1.0,0.0).astype(BF)
            sc=nt(jnp.concatenate([jnp.where(sel,qs,zero),eq],1),jnp.concatenate([k,kx],1))
            p=jnp.exp(sc)
            dp=nt(jnp.concatenate([jnp.where(sel,g,zero),gx],1),jnp.concatenate([v,vx],1))
            ds=(p*dp).astype(BF)
            ps.append(p.astype(BF)); ss.append(ds)
        kk=jnp.concatenate([jnp.where(even,k,zero),jnp.where(even,zero,k)],0)
        d_ref[:,cs]=(mm(jnp.concatenate(ss,1),kk)*0.125).astype(BF)
        qq=jnp.concatenate([jnp.where(even,q,zero),jnp.where(even,zero,q)],0)
        gg=jnp.concatenate([jnp.where(even,g,zero),jnp.where(even,zero,g)],0)
        d_ref[:,ck]=(tn(jnp.concatenate(ss,0),qq)*0.125).astype(BF)
        d_ref[:,cv]=tn(jnp.concatenate(ps,0),gg).astype(BF)
    u=colsum(d_ref[...].astype(F32))
    @pl.when(s==0)
    def _(): sm_ref[...]=u
    @pl.when(s>0)
    def _(): sm_ref[...]+=u


def attn_bwd(side,lengths,f,c,e,g):
    S=lengths.shape[0]; R=f.shape[0]; L=R//S
    rb=lambda n:pl.BlockSpec((L,n),lambda s,*_:(s,0))
    col=pl.BlockSpec((L,384),lambda s,*_:(s,side))
    return pl.pallas_call(attn_bwd_kernel,
        grid_spec=pltpu.PrefetchScalarGridSpec(num_scalar_prefetch=1,grid=(S,),
            in_specs=[rb(W3),col,rb(128),col],
            out_specs=[rb(W3),pl.BlockSpec((1,W3),lambda s,*_:(0,0))]),
        out_shape=[pltpu.HBM((R,W3),BF),jax.ShapeDtypeStruct((1,W3),F32)],
        compiler_params=pltpu.CompilerParams(vmem_limit_bytes=36<<20),
        cost_estimate=pl.CostEstimate(flops=8_000_000_000,bytes_accessed=12_000_000,transcendentals=3_500_000),
        name="attn_bwd")(lengths,*hbm(f,c,e,g))

def gelu_parts(v):
    phi=0.5+0.5*lax.erf(v*math.sqrt(0.5))
    return v*phi, phi+v*(jnp.exp(v*v*-0.5)*(1.0/math.sqrt(2*math.pi)))
def ln_parts(h):
    mu=jnp.mean(h,1,keepdims=True); c=h-mu
    r=lax.rsqrt(jnp.mean(c*c,1,keepdims=True)+EPS)
    return c*r, r
def ln_back(up,n,r,gain):
    e=up*gain
    return r*(e-jnp.mean(e,1,keepdims=True)-n*jnp.mean(e*n,1,keepdims=True))
def colsum(x): return jnp.sum(x,0,keepdims=True)
FC=512
def once(a,b): return pl.BlockSpec((a,b),lambda s,*_:(0,0),pipeline_mode=pl.Buffered(1))
def ffn_in_kernel(x_ref,c_ref,wo_ref,we_ref,sp_ref,be_ref,n1_ref,r1_ref,fl_ref,act_ref,gp_ref):
    M=x_ref.shape[0]; FF=we_ref.shape[1]
    sp=sp_ref[...].astype(F32)
    att=mm(c_ref[...],wo_ref[...])+sp[0:1]
    n1,r1=ln_parts(x_ref[...].astype(F32)+att)
    n1_ref[...]=n1; r1_ref[...]=jnp.broadcast_to(r1,(M,128))
    fl=(n1*sp[1:2]+sp[2:3]).astype(BF); fl_ref[...]=fl
    for f in range(0,FF,FC):
        fs=slice(f,f+FC)
        a,gp=gelu_parts(mm(fl,we_ref[:,fs])+be_ref[:,fs].astype(F32))
        act_ref[:,fs]=a.astype(BF); gp_ref[:,fs]=gp.astype(BF)

def ffn_in(x,c,wo,we,sp,be,S):
    R=x.shape[0]; M=R//S; FF=we.shape[1]
    rb=lambda n:pl.BlockSpec((M,n),lambda s,*_:(s,0))
    return pl.pallas_call(ffn_in_kernel,grid=(S,),
            in_specs=[rb(D),rb(D),RESIDENT,RESIDENT,once(8,D),once(1,FF)],
            out_specs=[rb(D),rb(128),rb(D),rb(FF),rb(FF)],
        out_shape=[pltpu.HBM((R,D),F32),pltpu.HBM((R,128),F32),pltpu.HBM((R,D),BF),
            pltpu.HBM((R,FF),BF),pltpu.HBM((R,FF),BF)],
        compiler_params=pltpu.CompilerParams(vmem_limit_bytes=40 << 20),
        cost_estimate=pl.CostEstimate(flops=9_000_000_000,bytes_accessed=40_000_000,transcendentals=9_000_000),
        name="ffn_in")(*hbm(x,c),*vmem(wo,we),sp,be)

def ffn_out_kernel(bk_ref,n1_ref,r1_ref,act_ref,gp_ref,go_ref,wo_ref,we_ref,ws_ref,sp_ref,
        out_ref,gs_ref,ge_ref,gr_ref,ga_ref,gc_ref,sm_ref,sb_ref):
    M=n1_ref.shape[0]; FF=we_ref.shape[1]
    s=pl.program_id(0)
    sp=sp_ref[...].astype(F32)
    bo,g1,s1,bs,g2,s2=[sp[i:i+1] for i in range(6)]
    n1=n1_ref[...]
    n2,r2=ln_parts((n1*g1+s1)+(mm(act_ref[...],ws_ref[...])+bs))
    rows=jnp.where(bk_ref[s]==0,176,jnp.where(bk_ref[s]==1,224,384))
    rm=jnp.where(lax.broadcasted_iota(jnp.int32,(M,1),0)<rows,1.0,0.0)
    out_ref[...]=((n2*g2+s2)*rm).astype(BF)
    up=go_ref[...].astype(F32)*rm
    gh=ln_back(up,n2,r2,g2)
    gs=gh.astype(BF); gs_ref[...]=gs
    acc=gh
    bsum=[]
    for f in range(0,FF,FC):
        fs=slice(f,f+FC)
        ge=(nt(gs,ws_ref[fs,:])*gp_ref[:,fs].astype(F32)).astype(BF)
        ge_ref[:,fs]=ge
        bsum.append(colsum(ge.astype(F32)))
        acc=acc+nt(ge,we_ref[:,fs])
    gr=ln_back(acc,n1,r1_ref[:,:1],g1)
    gr_ref[...]=gr
    ga=gr.astype(BF); ga_ref[...]=ga
    gc_ref[...]=nt(ga,wo_ref[...]).astype(BF)
    u=jnp.concatenate([colsum(ga.astype(F32)),colsum(acc*n1),colsum(acc),colsum(gs.astype(F32)),colsum(up*n2),colsum(up),jnp.zeros((2,D),F32)],0)
    ub=jnp.concatenate(bsum,1)
    @pl.when(s==0)
    def _():
        sm_ref[...]=u; sb_ref[...]=ub
    @pl.when(s>0)
    def _():
        sm_ref[...]+=u; sb_ref[...]+=ub

def ffn_out(buckets,n1,r1,act,gp,go,wo,we,ws,sp):
    S=buckets.shape[0]; R=n1.shape[0]; M=R//S; FF=we.shape[1]
    rb=lambda n:pl.BlockSpec((M,n),lambda s,*_:(s,0))
    full=lambda a,b:pl.BlockSpec((a,b),lambda s,*_:(0,0))
    return pl.pallas_call(ffn_out_kernel,
        grid_spec=pltpu.PrefetchScalarGridSpec(num_scalar_prefetch=1,grid=(S,),
            in_specs=[rb(D),rb(128),rb(FF),rb(FF),rb(D),RESIDENT,RESIDENT,RESIDENT,once(8,D)],
            out_specs=[rb(D),rb(D),rb(FF),rb(D),rb(D),rb(D),full(8,D),full(1,FF)]),
        out_shape=[pltpu.HBM((R,D),BF),pltpu.HBM((R,D),BF),pltpu.HBM((R,FF),BF),
            pltpu.HBM((R,D),F32),pltpu.HBM((R,D),BF),
            pltpu.HBM((R,D),BF),pltpu.HBM((8,D),F32),pltpu.HBM((1,FF),F32)],
        compiler_params=pltpu.CompilerParams(vmem_limit_bytes=48 << 20),
        cost_estimate=pl.CostEstimate(flops=24_000_000_000,bytes_accessed=60_000_000,transcendentals=0),
        name="ffn_out")(buckets,*hbm(n1,r1,act,gp,go),*vmem(wo,we,ws),sp)

def tn_kernel(a_ref,b_ref,o_ref): o_ref[...]=tn(a_ref[...],b_ref[...]).astype(o_ref.dtype)
def grad_w(a,b,bm,bn,name,dt=BF,order=0):
    R,Ma=a.shape; Nb=b.shape[1]
    if order==0:
        grid=(Ma//bm,Nb//bn); ia=lambda i,j:(0,i); ib=lambda i,j:(0,j); io=lambda i,j:(i,j)
    else:
        grid=(Nb//bn,Ma//bm); ia=lambda j,i:(0,i); ib=lambda j,i:(0,j); io=lambda j,i:(i,j)
    return pl.pallas_call(tn_kernel,grid=grid,in_specs=[pl.BlockSpec((R,bm),ia),pl.BlockSpec((R,bn),ib)],
        out_specs=pl.BlockSpec((bm,bn),io),out_shape=jax.ShapeDtypeStruct((Ma,Nb),dt),
        compiler_params=pltpu.CompilerParams(vmem_limit_bytes=VM),
        cost_estimate=pl.CostEstimate(flops=2*R*Ma*Nb,bytes_accessed=2*R*(Ma+Nb)+2*Ma*Nb,transcendentals=0),
        name=name)(a,b)
def resid_kernel(gr_ref,dl_ref,dh_ref,wl_ref,wh_ref,o_ref):
    o_ref[...]=gr_ref[...]+nt(dl_ref[...],wl_ref[:,:W3])+nt(dh_ref[...],wh_ref[...])

def grad_in(gr,dl,dh,wl,wh,S):
    R=gr.shape[0]; M=R//S
    rb=lambda n:pl.BlockSpec((M,n),lambda s:(s,0))
    return pl.pallas_call(resid_kernel,grid=(S,),in_specs=[rb(D),rb(W3),rb(W3),once(*wl.shape),once(*wh.shape)],out_specs=rb(D),
        out_shape=pltpu.HBM((R,D),F32),
        compiler_params=pltpu.CompilerParams(vmem_limit_bytes=48<<20),
        cost_estimate=pl.CostEstimate(flops=6*R*D*D,bytes_accessed=20_000_000,transcendentals=0),
        name="grad_in")(*hbm(gr,dl,dh),wl,wh)

def exchange(value, pairs):
    return lax.ppermute(value, "dp", pairs)


def flip(count, mask):
    return [(i, i ^ mask) for i in range(count)]


def turn(count, even_mask, odd_mask):
    return [(i, i ^ (odd_mask if i & 1 else even_mask)) for i in range(count)]


def along_z(block):
    return jnp.stack([block] + [exchange(block, flip(32, 8 * k)) for k in (1, 2, 3)])


def z_moves(block):
    return [block] + [exchange(block, flip(32, 8 * k)) for k in (1, 2, 3)]


def near(pieces):
    return exchange(pieces, turn(32, 2, 4))


def far(pieces):
    return exchange(pieces, turn(32, 4, 2))


def both_cores(*pieces):
    return pieces + tuple(exchange(piece, flip(32, 1)) for piece in pieces)


def together(*values):
    return lax.optimization_barrier(values)


def piece_owner(me, other_core, far, near, k):
    core = me & 1
    near_mask = 2 + 2 * (core ^ other_core)
    far_mask = 6 - near_mask
    return me ^ (other_core + far * far_mask + near * near_mask + 8 * k)


def unpack_kernel(cuts, wide, me_ref, *refs):
    pieces, outs, sems = refs[:6], refs[6:-1], refs[-1]
    me = me_ref[0]
    for other in (0, 1):
        along_z, near, far = pieces[3 * other : 3 * other + 3]
        for k in range(4):
            for ref, at, owner in (
                (along_z, k, piece_owner(me, other, 0, 0, k)),
                (near, k, piece_owner(me, other, 0, 1, k)),
                (far, k, piece_owner(me, other, 1, 0, k)),
                (far, 4 + k, piece_owner(me, other, 1, 1, k)),
            ):
                for i, start, rows, column in cuts:
                    pltpu.make_async_copy(
                        ref.at[at, pl.ds(start, rows)],
                        outs[i].at[owner, :, pl.ds(column, wide)],
                        sems.at[i],
                    ).start()
    for i, out in enumerate(outs):
        pltpu.make_async_copy(out, out, sems.at[i]).wait()


def unpack(me, pieces, sizes, name):
    cuts = []
    wide = pieces[0].shape[2]
    start = 0
    for i, (rows, columns) in enumerate(sizes):
        for column in range(0, columns, wide):
            cuts.append((i, start, rows, column))
            start += rows
    anywhere = pl.BlockSpec(memory_space=pl.ANY)
    return pl.pallas_call(
        functools.partial(unpack_kernel, tuple(cuts), wide),
        grid_spec=pltpu.PrefetchScalarGridSpec(
            num_scalar_prefetch=1,
            grid=(1,),
            in_specs=[anywhere] * 6,
            out_specs=[anywhere] * len(sizes),
            scratch_shapes=[pltpu.SemaphoreType.DMA((len(sizes),))],
        ),
        out_shape=[pltpu.VMEM((32, *size), BF) for size in sizes],
        compiler_params=pltpu.CompilerParams(vmem_limit_bytes=4 << 20),
        cost_estimate=pl.CostEstimate(
            flops=0, bytes_accessed=2 * 64 * wide * start, transcendentals=0
        ),
        name=name,
    )(me, *pieces)


def place(me, total, keep, send, at):
    for other, target in ((0, keep), (1, send)):
        for far in (0, 1):
            for near in (0, 1):
                for k in range(4):
                    owner = piece_owner(me, other, far, near, k)
                    rows = total[pl.ds(pl.multiple_of(24 * owner, 8), 24), :]
                    at(target, 8 * far + 4 * near + k, rows.astype(BF))


def dw_expand_kernel(me_ref, fl_ref, ge_ref, c_ref, ga_ref, keep, send, total):
    j = pl.program_id(0)

    @pl.when(j < 4)
    def _():
        total[...] = tn(fl_ref[...], ge_ref[...])

    @pl.when(j == 4)
    def _():
        total[...] = tn(c_ref[...], ga_ref[...])

    def at(ref, piece, rows):
        ref[piece, 0] = rows

    place(me_ref[0], total, keep, send, at)


def dw_expand_packed(me, first_low, grad_expand, context, grad_attended):
    R = first_low.shape[0]
    fixed = pl.BlockSpec((R, D), lambda j, *_: (0, 0), pipeline_mode=pl.Buffered(1))
    out = pl.BlockSpec((16, 1, 24, D), lambda j, *_: (0, j, 0, 0))
    return pl.pallas_call(
        dw_expand_kernel,
        grid_spec=pltpu.PrefetchScalarGridSpec(
            num_scalar_prefetch=1,
            grid=(5,),
            in_specs=[
                fixed,
                pl.BlockSpec((R, D), lambda j, *_: (0, jnp.minimum(j, 3))),
                fixed,
                fixed,
            ],
            out_specs=[out, out],
            scratch_shapes=[pltpu.VMEM((D, D), F32)],
        ),
        out_shape=[jax.ShapeDtypeStruct((16, 5, 24, D), BF)] * 2,
        compiler_params=pltpu.CompilerParams(vmem_limit_bytes=40 << 20),
        cost_estimate=pl.CostEstimate(
            flops=10 * R * D * D, bytes_accessed=22_000_000, transcendentals=0
        ),
        name="dw_expand",
    )(me, *hbm(first_low, grad_expand, context, grad_attended))


def dw_shrink_kernel(me_ref, a_ref, gs_ref, keep, send, total):
    me = me_ref[0]
    core = me & 1
    i = pl.program_id(0)
    total[...] = tn(a_ref[...], gs_ref[...])
    for pair in range(4):
        for other, target in ((0, keep), (1, send)):
            local = 2 * pair + (core ^ other)
            away = (8 * i + local) ^ me ^ other
            side = core ^ other
            near = (away >> (1 + side)) & 1
            far = (away >> (2 - side)) & 1
            piece = 8 * far + 4 * near + (away >> 3)
            rows = total[pl.ds(pl.multiple_of(96 * local, 8), 96), :].astype(BF)
            target[piece] = rows


def dw_shrink_packed(me, active, grad_shrink):
    R = active.shape[0]
    out = pl.BlockSpec((16, 96, D), lambda i, *_: (0, 0, 0))
    return pl.pallas_call(
        dw_shrink_kernel,
        grid_spec=pltpu.PrefetchScalarGridSpec(
            num_scalar_prefetch=1,
            grid=(4,),
            in_specs=[
                pl.BlockSpec((R, D), lambda i, *_: (0, i)),
                pl.BlockSpec((R, D), lambda i, *_: (0, 0), pipeline_mode=pl.Buffered(1)),
            ],
            out_specs=[out, out],
            scratch_shapes=[pltpu.VMEM((D, D), F32)],
        ),
        out_shape=[jax.ShapeDtypeStruct((16, 96, D), BF)] * 2,
        compiler_params=pltpu.CompilerParams(vmem_limit_bytes=40 << 20),
        cost_estimate=pl.CostEstimate(
            flops=8 * R * D * D, bytes_accessed=17_000_000, transcendentals=0
        ),
        name="dw_shrink",
    )(me, *hbm(active, grad_shrink))


def dw_qkv_kernel(me_ref, x_ref, lo_ref, hi_ref, rows_ref, keep, send, total):
    me = me_ref[0]
    j = pl.program_id(0)

    for unit, ref in ((0, lo_ref), (1, hi_ref)):

        @pl.when(j == unit)
        def _():
            total[...] = tn(x_ref[...], ref[...])

            def at(target, piece, rows):
                target[piece, :, W3 * unit : W3 * unit + W3] = rows

            place(me, total, keep, send, at)

    @pl.when(j == 1)
    def _():
        for other, target in ((0, keep), (1, send)):
            for far in (0, 1):
                for near in (0, 1):
                    for k in range(4):
                        owner = piece_owner(me, other, far, near, k)
                        target[8 * far + 4 * near + k, :, 2 * W3 :] = rows_ref[owner]


def dw_qkv_packed(me, tokens, low, high, rows):
    R = tokens.shape[0]
    out = pl.BlockSpec((16, 24, 2 * W3 + 128), lambda j, *_: (0, 0, 0))
    fixed = lambda n: pl.BlockSpec((R, n), lambda j, *_: (0, 0), pipeline_mode=pl.Buffered(1))
    return pl.pallas_call(
        dw_qkv_kernel,
        grid_spec=pltpu.PrefetchScalarGridSpec(
            num_scalar_prefetch=1,
            grid=(2,),
            in_specs=[
                fixed(D),
                fixed(W3),
                fixed(W3),
                pl.BlockSpec((32, 24, 128), lambda j, *_: (0, 0, 0)),
            ],
            out_specs=[out, out],
            scratch_shapes=[pltpu.VMEM((D, W3), F32)],
        ),
        out_shape=[jax.ShapeDtypeStruct((16, 24, 2 * W3 + 128), BF)] * 2,
        compiler_params=pltpu.CompilerParams(vmem_limit_bytes=48 << 20),
        cost_estimate=pl.CostEstimate(
            flops=6 * R * D * D, bytes_accessed=13_000_000, transcendentals=0
        ),
        name="dw_qkv",
    )(me, *hbm(tokens, low, high), rows)


def first_kernel(*refs):
    query, key, value, *vectors, expand, low, high = refs
    for side, out in ((0, low), (1, high)):
        for i, ref in enumerate((query, key, value)):
            out[:, 384 * i : 384 * i + 384] = ref[:, 384 * side : 384 * side + 384]
    low[:, W3:] = jnp.zeros((24, 128), BF)
    for i, vector in enumerate(vectors):
        low[i : i + 1, W3 : W3 + 24] = vector[...]
    low[8:9, W3 : W3 + 96] = expand[...]


def first_blocks(query, key, value, vectors, expand):
    return pl.pallas_call(
        first_kernel,
        out_shape=[jax.ShapeDtypeStruct((24, n), BF) for n in (WP, W3)],
        name="first_blocks",
    )(query, key, value, *[v[None] for v in vectors], expand[None])


def add_up(*parts):
    total = parts[0].astype(F32)
    for part in parts[1:]:
        total = total + part.astype(F32)
    return total


def halves(kept, came):
    n = kept.shape[0] // 2
    return (
        add_up(kept[:n], came[:n]).astype(BF),
        add_up(kept[n:], came[n:]).astype(BF),
    )


def quarters(kept, came):
    return [add_up(kept[k], came[k]).astype(BF) for k in range(4)]


def lines_of(parts):
    return [parts[0]] + [exchange(parts[k], flip(32, 8 * k)) for k in (1, 2, 3)]


def body(
    tokens,
    buckets,
    lengths,
    w_query,
    w_key,
    w_value,
    w_output,
    bias_query,
    bias_value,
    bias_output,
    gain_first,
    shift_first,
    w_expand,
    bias_expand,
    w_shrink,
    bias_shrink,
    gain_second,
    shift_second,
    grad_out,
    count,
):
    slots = buckets.shape[0]
    whole = lambda v: lax.all_gather(v, "dp", axis=0, tiled=True)
    short = (
        bias_output,
        gain_first,
        shift_first,
        bias_shrink,
        gain_second,
        shift_second,
        bias_query,
        bias_value,
    )
    tree = count == 32
    if tree:
        me = lax.axis_index("dp").astype(jnp.int32).reshape(1)
        block_l, block_h = first_blocks(w_query, w_key, w_value, short, bias_expand)
        block_b = jnp.concatenate(
            [w_output] + [w_expand[:, D * i : D * i + D] for i in range(4)]
        )
        line_l = along_z(block_l)
        line_l, block_h = together(line_l, block_h)
        near_l = near(line_l)
        line_h = z_moves(block_h)
        near_l, block_b, *line_h = together(near_l, block_b, *line_h)
        line_h = jnp.stack(line_h)
        far_l = far(jnp.concatenate([line_l, near_l]))
        near_h = near(line_h)
        line_b = z_moves(block_b)
        far_l, near_h, *line_b = together(far_l, near_h, *line_b)
        line_b = jnp.stack(line_b)
        far_h = far(jnp.concatenate([line_h, near_h]))
        (full_low,) = unpack(me, both_cores(line_l, near_l, far_l), ((24, WP),), "unpack_low")
        full_low = full_low.reshape(D, WP)
        rows = full_low[:, W3:].reshape(32, 24, 128)
        vectors = rows[:, :8, :24].transpose(1, 0, 2).reshape(8, D)
        full_bias_expand = rows[:, 8, :96].reshape(1, 4 * D)
        near_b = near(line_b)
        low, context, ends = attn_fwd(0, lengths, tokens, full_low, vectors)
        ends, far_h, near_b, block_c = together(ends, far_h, near_b, w_shrink)
        line_c = z_moves(block_c)
        (full_high,) = unpack(
            me, both_cores(line_h, near_h, far_h), ((24, W3),), "unpack_high"
        )
        full_high = full_high.reshape(D, W3)
        far_b_in = jnp.concatenate([line_b, near_b])
        vectors, far_b_in = together(vectors, far_b_in)
        far_b = far(far_b_in)
        high, context, ends_high = attn_fwd(
            1, lengths, tokens, full_high, vectors, context
        )
        far_b, ends_high, *line_c = together(far_b, ends_high, *line_c)
        line_c = jnp.stack(line_c)
        near_c = near(line_c)
        far_c_in = jnp.concatenate([line_c, near_c])
        full_bias_expand, far_c_in = together(full_bias_expand, far_c_in)
        full_output, full_expand = unpack(
            me, both_cores(line_b, near_b, far_b), ((24, D), (24, 4 * D)), "unpack_expand"
        )
        far_c = far(far_c_in)
        full_output = full_output.reshape(D, D)
        full_expand = full_expand.reshape(D, 4 * D)
    else:
        sides = lambda i: [w[:, 384 * i : 384 * i + 384] for w in (w_query, w_key, w_value)]
        full_low, full_high, full_output, full_expand, full_shrink = [
            whole(w)
            for w in (
                jnp.concatenate(sides(0), 1),
                jnp.concatenate(sides(1), 1),
                w_output,
                w_expand,
                w_shrink,
            )
        ]
        vectors = jnp.stack([whole(v) for v in short])
        full_bias_expand = whole(bias_expand)[None]
        low, context, ends = attn_fwd(0, lengths, tokens, full_low, vectors)
        high, context, ends_high = attn_fwd(
            1, lengths, tokens, full_high, vectors, context
        )

    normed, root, first_low, active, slope = ffn_in(
        tokens, context, full_output, full_expand, vectors, full_bias_expand, slots
    )
    if tree:
        far_c, normed = together(far_c, normed)
        (full_shrink,) = unpack(
            me, both_cores(line_c, near_c, far_c), ((96, D),), "unpack_shrink"
        )
        full_shrink = full_shrink.reshape(4 * D, D)
    (
        layer_out,
        grad_shrink,
        grad_expand,
        grad_h1,
        grad_attended,
        grad_context,
        sums_a,
        d_bias_expand,
    ) = ffn_out(
        buckets,
        normed,
        root,
        active,
        slope,
        grad_out,
        full_output,
        full_expand,
        full_shrink,
        vectors,
    )
    if tree:
        keep_b, send_b = dw_expand_packed(
            me, first_low, grad_expand, context, grad_attended
        )
        keep_b, send_b, active, grad_context = together(keep_b, send_b, active, grad_context)
        came_b = exchange(send_b, flip(32, 1))
        keep_c, send_c = dw_shrink_packed(me, active, grad_shrink)
        keep_c, send_c, came_b, grad_context = together(keep_c, send_c, came_b, grad_context)
        stay_b, go_b = halves(keep_b, came_b)
        stay_b, go_b, send_c, grad_context = together(stay_b, go_b, send_c, grad_context)
        came_b = far(go_b)
        came_c = exchange(send_c, flip(32, 1))
        grads_low, sums_b = attn_bwd(0, lengths, low, context, ends, grad_context)
        sums_b, came_b, came_c = together(sums_b, came_b, came_c)
        stay_b, go_b = halves(stay_b, came_b)
        stay_c, go_c = halves(keep_c, came_c)
        grad_context, sums_b, stay_b, stay_c, go_b, go_c = together(
            grad_context, sums_b, stay_b, stay_c, go_b, go_c
        )
        came_b = near(go_b)
        came_c = far(go_c)
        grads_high, sums_c = attn_bwd(
            1, lengths, high, context, ends_high, grad_context
        )
        sums_c, came_b, came_c = together(sums_c, came_b, came_c)
        parts_b = quarters(stay_b, came_b)
        stay_c, go_c = halves(stay_c, came_c)
        sides = lambda i: jnp.concatenate([sums_b[:, i : i + 384], sums_c[:, i : i + 384]], 1)
        rows = jnp.concatenate([sums_a[:6], sides(0), sides(768)])
        rows = rows.reshape(8, 32, 24).transpose(1, 0, 2)
        rows = jnp.pad(rows, ((0, 0), (0, 16), (0, 104))) + jnp.pad(
            d_bias_expand.reshape(32, 1, 96), ((0, 0), (8, 15), (0, 32))
        )
        rows = rows.astype(BF)
        rows, stay_c, go_c, *parts_b = together(rows, stay_c, go_c, *parts_b)
        came_c = near(go_c)
        lines_b = lines_of(parts_b)
        keep_a, send_a = dw_qkv_packed(me, tokens, grads_low, grads_high, rows)
        keep_a, send_a, came_c, *lines_b = together(keep_a, send_a, came_c, *lines_b)
        came_a = exchange(send_a, flip(32, 1))
        parts_c = quarters(stay_c, came_c)
        came_a, *parts_c = together(came_a, *parts_c)
        stay_a, go_a = halves(keep_a, came_a)
        stay_a, go_a, grad_h1, *parts_c = together(stay_a, go_a, grad_h1, *parts_c)
        came_a = far(go_a)
        lines_c = lines_of(parts_c)
    else:
        dw_expand = grad_w(first_low, grad_expand, 768, 768, "dw_expand")
        dw_output = grad_w(context, grad_attended, 768, 384, "dw_output")
        dw_shrink = grad_w(active, grad_shrink, 768, 768, "dw_shrink")
        grads_low, sums_b = attn_bwd(0, lengths, low, context, ends, grad_context)
        grads_high, sums_c = attn_bwd(
            1, lengths, high, context, ends_high, grad_context
        )
        dw_low = grad_w(tokens, grads_low, 768, 384, "dw_low")
        dw_high = grad_w(tokens, grads_high, 768, 384, "dw_high")
        sums = [sums_a[i] for i in range(6)] + [
            jnp.concatenate([sums_b[0, i : i + 384], sums_c[0, i : i + 384]])
            for i in (0, 768)
        ]
    grad_tokens = grad_in(
        grad_h1, grads_low, grads_high, full_low, full_high, slots
    )
    if tree:
        grad_tokens, came_a, *lines_c = together(grad_tokens, came_a, *lines_c)
        stay_a, go_a = halves(stay_a, came_a)
        stay_a, go_a = together(stay_a, go_a)
        came_a = near(go_a)
        sum_b = add_up(*lines_b)
        sum_c = add_up(*lines_c)
        sum_a = add_up(*lines_of(quarters(stay_a, came_a)))
        own_query, own_key, own_value = [
            jnp.concatenate([sum_a[:, i : i + 384], sum_a[:, W3 + i : W3 + i + 384]], 1)
            for i in (0, 384, 768)
        ]
        own_output = sum_b[4]
        own_expand = jnp.concatenate([sum_b[i] for i in range(4)], 1)
        own_shrink = sum_c
        own_rows = sum_a[:, 2 * W3 :]
        own_short = [own_rows[i, :24] for i in range(8)]
        own_bias_expand = own_rows[8, :96]
    else:
        owned = lambda v: lax.psum_scatter(
            v.astype(F32), "dp", scatter_dimension=0, tiled=True
        )
        own_output, own_expand, own_shrink, own_low, own_high = [
            owned(w) for w in (dw_output, dw_expand, dw_shrink, dw_low, dw_high)
        ]
        own_query, own_key, own_value = [
            jnp.concatenate([own_low[:, i : i + 384], own_high[:, i : i + 384]], 1)
            for i in (0, 384, 768)
        ]
        own_short = [owned(v) for v in sums]
        own_bias_expand = owned(d_bias_expand[0])
    (
        own_bias_output,
        own_gain_first,
        own_shift_first,
        own_bias_shrink,
        own_gain_second,
        own_shift_second,
        own_bias_query,
        own_bias_value,
    ) = own_short
    return (
        layer_out,
        grad_tokens,
        own_query,
        own_key,
        own_value,
        own_output,
        own_bias_query,
        own_bias_value,
        own_bias_output,
        own_gain_first,
        own_shift_first,
        own_expand,
        own_bias_expand,
        own_shrink,
        own_bias_shrink,
        own_gain_second,
        own_shift_second,
    )


def solution(mesh):
    split = P("dp")
    wide = P("dp", None)
    return jax.shard_map(
        functools.partial(body, count=mesh.shape["dp"]),
        mesh=mesh,
        in_specs=(wide, split, split)
        + (wide,) * 4
        + (split,) * 5
        + (wide, split, wide, split, split, split, wide),
        out_specs=(wide,) * 6 + (split,) * 5 + (wide, split, wide, split, split, split),
        check_vma=False,
    )
```

```python
import functools, math
import jax, jax.numpy as jnp
from jax import lax
from jax.experimental import pallas as pl
from jax.experimental.pallas import tpu as pltpu
from jax.sharding import PartitionSpec as P
BF=jnp.bfloat16; F32=jnp.float32
D=768; HD=64; PAIRS=6
VM=58<<20
NEG=-1e30
def hbm(*arrays): return [pltpu.with_memory_space_constraint(a,pltpu.HBM) for a in arrays]
def vmem(*arrays): return [pltpu.with_memory_space_constraint(a,pltpu.VMEM) for a in arrays]
RESIDENT=pl.BlockSpec(memory_space=pltpu.VMEM)
def mm(a,b): return lax.dot_general(a,b,(((1,),(0,)),((),())),preferred_element_type=F32)
def nt(a,b): return lax.dot_general(a,b,(((1,),(1,)),((),())),preferred_element_type=F32)
def tn(a,b): return lax.dot_general(a,b,(((0,),(0,)),((),())),preferred_element_type=F32)
def lanes(rows,n=128): return lax.broadcasted_iota(jnp.int32,(rows,n),1)

def attn_fwd_kernel(lo, len_ref, x_ref, wq_ref, wk_ref, wv_ref, sp_ref, q_ref, k_ref, v_ref, c_ref, e_ref):
    L=x_ref.shape[0]
    n=len_ref[pl.program_id(0)+lo]
    x=x_ref[...]
    q=(mm(x,wq_ref[...])+sp_ref[6:7].astype(F32)).astype(BF)
    k=mm(x,wk_ref[...]).astype(BF)
    v=(mm(x,wv_ref[...])+sp_ref[7:8].astype(F32)).astype(BF)
    q_ref[...]=q; k_ref[...]=k; v_ref[...]=v
    ln=lanes(L)
    even=ln<64
    row=lax.broadcasted_iota(jnp.int32,(L,128),0)
    kx=jnp.where((ln==0)&(row>=n),NEG,0.0).astype(BF)
    qx=jnp.where(ln==0,1.0,0.0).astype(BF)
    one_e=jnp.where(even,1.0,0.0).astype(BF)
    one_o=jnp.where(even,0.0,1.0).astype(BF)
    zero=jnp.zeros((L,128),BF)
    mt=jnp.zeros((L,128),F32); lt=jnp.ones((L,128),F32)
    for t in range(PAIRS):
        cs=slice(128*t,128*t+128)
        qp=q[:,cs]*jnp.asarray(0.125,BF); kp=k[:,cs]; vp=v[:,cs]
        ke=jnp.concatenate([kp,kx],1)
        ps=[];ms=[]
        for o in (0,1):
            qm=jnp.where(even if o==0 else ~even, qp, zero)
            sc=nt(jnp.concatenate([qm,qx],1),ke)
            m=jnp.max(sc,1,keepdims=True)
            ps.append(jnp.exp(sc-m).astype(BF)); ms.append(m)
        vv=jnp.concatenate([jnp.concatenate([jnp.where(even,vp,zero),one_e],1),
                            jnp.concatenate([jnp.where(even,zero,vp),one_o],1)],0)
        r=mm(jnp.concatenate(ps,1),vv)
        lb=r[:,128:]
        c_ref[:,cs]=(r[:,:128]/lb).astype(BF)
        sel_e=ln==t; sel_o=ln==64+t
        mt=jnp.where(sel_e,ms[0],jnp.where(sel_o,ms[1],mt))
        lt=jnp.where(sel_e|sel_o,lb,lt)
    neg=-(mt+jnp.log(lt))
    hi=neg.astype(BF); r1=neg-hi.astype(F32)
    mid=r1.astype(BF); rest=(r1-mid.astype(F32)).astype(BF)
    use=(ln%64)<PAIRS
    z=jnp.zeros((L,128),F32)
    e=jnp.where(use,hi.astype(F32),z)+pltpu.roll(jnp.where(use,mid.astype(F32),z),8,1)+pltpu.roll(jnp.where(use,rest.astype(F32),z),16,1)
    e=jnp.where(ln==24,1.0,e)
    e_ref[...]=e.astype(BF)

def over_slots(kernel,nin,lo,before):
    n=len(before)
    def run(*refs): kernel(lo,*refs[:nin],*refs[nin+n:])
    return run,[pl.BlockSpec(memory_space=pl.ANY)]*n,{nin+i:i for i in range(n)}

def attn_fwd(lengths,x,wq,wk,wv,sp,lo,hi,before=()):
    S=lengths.shape[0]; R=x.shape[0]; L=R//S
    rowb=pl.BlockSpec((L,D),lambda s,*_:(s+lo,0))
    kern,extra,alias=over_slots(attn_fwd_kernel,6,lo,before)
    b=pl.BlockSpec((8,D),lambda s,*_:(0,0))
    return pl.pallas_call(kern,
        grid_spec=pltpu.PrefetchScalarGridSpec(num_scalar_prefetch=1,grid=(hi-lo,),
            in_specs=[rowb,RESIDENT,RESIDENT,RESIDENT,b]+extra,
            out_specs=[rowb,rowb,rowb,rowb,pl.BlockSpec((L,128),lambda s,*_:(s+lo,0))]),
        input_output_aliases=alias,
        out_shape=[pltpu.HBM((R,D),BF)]*4+[pltpu.HBM((R,128),BF)],
        compiler_params=pltpu.CompilerParams(vmem_limit_bytes=30 << 20),
        cost_estimate=pl.CostEstimate(flops=2_500_000_000*(hi-lo),bytes_accessed=5_000_000*(hi-lo),transcendentals=1_700_000*(hi-lo)),
        name="attn_fwd")(lengths,*hbm(x),*vmem(wq,wk,wv),sp,*before)

def attn_bwd_kernel(lo, len_ref, q_ref, k_ref, v_ref, c_ref, e_ref, g_ref, d_ref, sm_ref):
    L=q_ref.shape[0]
    s=pl.program_id(0)
    n=len_ref[s+lo]
    ln=lanes(L); even=ln<64
    row=lax.broadcasted_iota(jnp.int32,(L,128),0)
    eq=e_ref[...]
    mask=(ln==24)&(row>=n)
    zero=jnp.zeros((L,128),BF); zf=jnp.zeros((L,128),F32)
    scale=jnp.asarray(0.125,BF)
    kbase=jnp.where(mask,NEG,0.0)
    for t in range(PAIRS):
        cs=slice(128*t,128*t+128)
        q=q_ref[:,cs]; k=k_ref[:,cs]; v=v_ref[:,cs]; g=g_ref[:,cs]
        qs=q*scale
        gc=g.astype(F32)*c_ref[:,cs].astype(F32)
        ps=[];ss=[]
        for o in (0,1):
            sel=even if o==0 else ~even
            d=jnp.sum(jnp.where(sel,gc,zf),1,keepdims=True)
            dh=d.astype(BF).astype(F32); dl=d-dh
            gx=jnp.where(ln==0,-dh,jnp.where(ln==1,-dl,zf)).astype(BF)
            base=64*o+t
            hot=(ln==base)|(ln==base+8)|(ln==base+16)
            kx=jnp.where(hot,1.0,kbase).astype(BF)
            vx=jnp.where(ln<2,1.0,0.0).astype(BF)
            sc=nt(jnp.concatenate([jnp.where(sel,qs,zero),eq],1),jnp.concatenate([k,kx],1))
            p=jnp.exp(sc)
            dp=nt(jnp.concatenate([jnp.where(sel,g,zero),gx],1),jnp.concatenate([v,vx],1))
            ds=(p*dp).astype(BF)
            ps.append(p.astype(BF)); ss.append(ds)
        kk=jnp.concatenate([jnp.where(even,k,zero),jnp.where(even,zero,k)],0)
        d_ref[0,:,cs]=(mm(jnp.concatenate(ss,1),kk)*0.125).astype(BF)
        qq=jnp.concatenate([jnp.where(even,q,zero),jnp.where(even,zero,q)],0)
        gg=jnp.concatenate([jnp.where(even,g,zero),jnp.where(even,zero,g)],0)
        d_ref[1,:,cs]=(tn(jnp.concatenate(ss,0),qq)*0.125).astype(BF)
        d_ref[2,:,cs]=tn(jnp.concatenate(ps,0),gg).astype(BF)
    u=jnp.concatenate([colsum(d_ref[0].astype(F32)),colsum(d_ref[2].astype(F32)),jnp.zeros((6,D),F32)],0)
    @pl.when(s==0)
    def _(): sm_ref[...]=u
    @pl.when(s>0)
    def _(): sm_ref[...]+=u

def attn_bwd(lengths,q,k,v,c,e,g,lo,hi,before=()):
    S=lengths.shape[0]; R=q.shape[0]; L=R//S
    rowb=pl.BlockSpec((L,D),lambda s,*_:(s+lo,0))
    kern,extra,alias=over_slots(attn_bwd_kernel,7,lo,before)
    return pl.pallas_call(kern,
        grid_spec=pltpu.PrefetchScalarGridSpec(num_scalar_prefetch=1,grid=(hi-lo,),
            in_specs=[rowb,rowb,rowb,rowb,pl.BlockSpec((L,128),lambda s,*_:(s+lo,0)),rowb]+extra,
            out_specs=[pl.BlockSpec((3,L,D),lambda s,*_:(0,s+lo,0)),pl.BlockSpec((8,D),lambda s,*_:(0,0))]),
        input_output_aliases=alias,
        out_shape=[pltpu.HBM((3,R,D),BF),jax.ShapeDtypeStruct((8,D),F32)],
        compiler_params=pltpu.CompilerParams(vmem_limit_bytes=36 << 20),
        cost_estimate=pl.CostEstimate(flops=4_000_000_000*(hi-lo),bytes_accessed=6_000_000*(hi-lo),transcendentals=1_700_000*(hi-lo)),
        name="attn_bwd")(lengths,*hbm(q,k,v,c,e,g),*before)

EPS=1e-12
def gelu_parts(v):
    phi=0.5+0.5*lax.erf(v*math.sqrt(0.5))
    return v*phi, phi+v*(jnp.exp(v*v*-0.5)*(1.0/math.sqrt(2*math.pi)))
def ln_parts(h):
    mu=jnp.mean(h,1,keepdims=True); c=h-mu
    r=lax.rsqrt(jnp.mean(c*c,1,keepdims=True)+EPS)
    return c*r, r
def ln_back(up,n,r,gain):
    e=up*gain
    return r*(e-jnp.mean(e,1,keepdims=True)-n*jnp.mean(e*n,1,keepdims=True))
def colsum(x): return jnp.sum(x,0,keepdims=True)
FC=1536
def once(a,b): return pl.BlockSpec((a,b),lambda s,*_:(0,0),pipeline_mode=pl.Buffered(1))
def ffn_in_kernel(x_ref,c_ref,wo_ref,we_ref,sp_ref,be_ref,n1_ref,r1_ref,fl_ref,act_ref,gp_ref):
    M=x_ref.shape[0]; FF=we_ref.shape[1]
    sp=sp_ref[...].astype(F32)
    att=mm(c_ref[...],wo_ref[...])+sp[0:1]
    n1,r1=ln_parts(x_ref[...].astype(F32)+att)
    n1_ref[...]=n1; r1_ref[...]=jnp.broadcast_to(r1,(M,128))
    fl=(n1*sp[1:2]+sp[2:3]).astype(BF); fl_ref[...]=fl
    for f in range(0,FF,FC):
        fs=slice(f,f+FC)
        a,gp=gelu_parts(mm(fl,we_ref[:,fs])+be_ref[:,fs].astype(F32))
        act_ref[:,fs]=a.astype(BF); gp_ref[:,fs]=gp.astype(BF)

def ffn_in(x,c,wo,we,sp,be,S):
    R=x.shape[0]; M=R//S; FF=we.shape[1]
    rb=lambda n:pl.BlockSpec((M,n),lambda s,*_:(s,0))
    return pl.pallas_call(ffn_in_kernel,grid=(S,),
            in_specs=[rb(D),rb(D),RESIDENT,RESIDENT,once(8,D),once(1,FF)],
            out_specs=[rb(D),rb(128),rb(D),rb(FF),rb(FF)],
        out_shape=[pltpu.HBM((R,D),F32),pltpu.HBM((R,128),F32),pltpu.HBM((R,D),BF),
            pltpu.HBM((R,FF),BF),pltpu.HBM((R,FF),BF)],
        compiler_params=pltpu.CompilerParams(vmem_limit_bytes=40 << 20),
        cost_estimate=pl.CostEstimate(flops=9_000_000_000,bytes_accessed=40_000_000,transcendentals=9_000_000),
        name="ffn_in")(*hbm(x,c),*vmem(wo,we),sp,be)

def ffn_out_kernel(bk_ref,n1_ref,r1_ref,act_ref,gp_ref,go_ref,wo_ref,we_ref,ws_ref,sp_ref,
        out_ref,gs_ref,ge_ref,gr_ref,ga_ref,gc_ref,sm_ref,sb_ref):
    M=n1_ref.shape[0]; FF=we_ref.shape[1]
    s=pl.program_id(0)
    sp=sp_ref[...].astype(F32)
    bo,g1,s1,bs,g2,s2=[sp[i:i+1] for i in range(6)]
    n1=n1_ref[...]
    n2,r2=ln_parts((n1*g1+s1)+(mm(act_ref[...],ws_ref[...])+bs))
    rows=jnp.where(bk_ref[s]==0,176,jnp.where(bk_ref[s]==1,224,384))
    rm=jnp.where(lax.broadcasted_iota(jnp.int32,(M,1),0)<rows,1.0,0.0)
    out_ref[...]=((n2*g2+s2)*rm).astype(BF)
    up=go_ref[...].astype(F32)*rm
    gh=ln_back(up,n2,r2,g2)
    gs=gh.astype(BF); gs_ref[...]=gs
    acc=gh
    bsum=[]
    for f in range(0,FF,FC):
        fs=slice(f,f+FC)
        ge=(nt(gs,ws_ref[fs,:])*gp_ref[:,fs].astype(F32)).astype(BF)
        ge_ref[:,fs]=ge
        bsum.append(colsum(ge.astype(F32)))
        acc=acc+nt(ge,we_ref[:,fs])
    gr=ln_back(acc,n1,r1_ref[:,:1],g1)
    gr_ref[...]=gr
    ga=gr.astype(BF); ga_ref[...]=ga
    gc_ref[...]=nt(ga,wo_ref[...]).astype(BF)
    u=jnp.concatenate([colsum(ga.astype(F32)),colsum(acc*n1),colsum(acc),colsum(gs.astype(F32)),colsum(up*n2),colsum(up),jnp.zeros((2,D),F32)],0)
    ub=jnp.concatenate(bsum,1)
    @pl.when(s==0)
    def _():
        sm_ref[...]=u; sb_ref[...]=ub
    @pl.when(s>0)
    def _():
        sm_ref[...]+=u; sb_ref[...]+=ub

def ffn_out(buckets,n1,r1,act,gp,go,wo,we,ws,sp):
    S=buckets.shape[0]; R=n1.shape[0]; M=R//S; FF=we.shape[1]
    rb=lambda n:pl.BlockSpec((M,n),lambda s,*_:(s,0))
    full=lambda a,b:pl.BlockSpec((a,b),lambda s,*_:(0,0))
    return pl.pallas_call(ffn_out_kernel,
        grid_spec=pltpu.PrefetchScalarGridSpec(num_scalar_prefetch=1,grid=(S,),
            in_specs=[rb(D),rb(128),rb(FF),rb(FF),rb(D),RESIDENT,RESIDENT,RESIDENT,once(8,D)],
            out_specs=[rb(D),rb(D),rb(FF),rb(D),rb(D),rb(D),full(8,D),full(1,FF)]),
        out_shape=[pltpu.HBM((R,D),BF),pltpu.HBM((R,D),BF),pltpu.HBM((R,FF),BF),
            pltpu.HBM((R,D),F32),pltpu.HBM((R,D),BF),
            pltpu.HBM((R,D),BF),pltpu.HBM((8,D),F32),pltpu.HBM((1,FF),F32)],
        compiler_params=pltpu.CompilerParams(vmem_limit_bytes=48 << 20),
        cost_estimate=pl.CostEstimate(flops=24_000_000_000,bytes_accessed=60_000_000,transcendentals=0),
        name="ffn_out")(buckets,*hbm(n1,r1,act,gp,go),*vmem(wo,we,ws),sp)

def tn_kernel(a_ref,b_ref,o_ref): o_ref[...]=tn(a_ref[...],b_ref[...]).astype(o_ref.dtype)
def grad_w(a,b,bm,bn,name,dt=BF,order=0):
    R,Ma=a.shape; Nb=b.shape[1]
    if order==0:
        grid=(Ma//bm,Nb//bn); ia=lambda i,j:(0,i); ib=lambda i,j:(0,j); io=lambda i,j:(i,j)
    else:
        grid=(Nb//bn,Ma//bm); ia=lambda j,i:(0,i); ib=lambda j,i:(0,j); io=lambda j,i:(i,j)
    return pl.pallas_call(tn_kernel,grid=grid,in_specs=[pl.BlockSpec((R,bm),ia),pl.BlockSpec((R,bn),ib)],
        out_specs=pl.BlockSpec((bm,bn),io),out_shape=jax.ShapeDtypeStruct((Ma,Nb),dt),
        compiler_params=pltpu.CompilerParams(vmem_limit_bytes=VM),
        cost_estimate=pl.CostEstimate(flops=2*R*Ma*Nb,bytes_accessed=2*R*(Ma+Nb)+2*Ma*Nb,transcendentals=0),
        name=name)(a,b)
def resid_kernel(gr_ref,d_ref,wa_ref,wb_ref,wc_ref,o_ref):
    o_ref[...]=gr_ref[...]+nt(d_ref[0],wa_ref[...])+nt(d_ref[1],wb_ref[...])+nt(d_ref[2],wc_ref[...])
def grad_in(gr,d,wa,wb,wc,S):
    R=gr.shape[0]; M=R//S
    rb=pl.BlockSpec((M,D),lambda s:(s,0))
    return pl.pallas_call(resid_kernel,grid=(S,),in_specs=[rb,pl.BlockSpec((3,M,D),lambda s:(0,s,0))]+[RESIDENT]*3,out_specs=rb,
        out_shape=pltpu.HBM((R,D),F32),
        compiler_params=pltpu.CompilerParams(vmem_limit_bytes=30 << 20),
        cost_estimate=pl.CostEstimate(flops=6*R*D*D,bytes_accessed=20_000_000,transcendentals=0),
        name="grad_in")(*hbm(gr,d),wa,wb,wc)

def exchange(value, pairs):
    return lax.ppermute(value, "dp", pairs)


def flip(count, mask):
    return [(i, i ^ mask) for i in range(count)]


def turn(count, even_mask, odd_mask):
    return [(i, i ^ (odd_mask if i & 1 else even_mask)) for i in range(count)]


def along_z(block):
    return jnp.stack([block] + [exchange(block, flip(32, 8 * k)) for k in (1, 2, 3)])


def near(pieces):
    return exchange(pieces, turn(32, 2, 4))


def far(pieces):
    return exchange(pieces, turn(32, 4, 2))


def both_cores(*pieces):
    return pieces + tuple(exchange(piece, flip(32, 1)) for piece in pieces)


def together(*values):
    return lax.optimization_barrier(values)


def piece_owner(me, other_core, far, near, k):
    core = me & 1
    near_mask = 2 + 2 * (core ^ other_core)
    far_mask = 6 - near_mask
    return me ^ (other_core + far * far_mask + near * near_mask + 8 * k)


def unpack_kernel(cuts, me_ref, *refs):
    pieces, outs, sems = refs[:6], refs[6:-1], refs[-1]
    me = me_ref[0]
    for other in (0, 1):
        along_z, near, far = pieces[3 * other : 3 * other + 3]
        for k in range(4):
            for ref, at, owner in (
                (along_z, k, piece_owner(me, other, 0, 0, k)),
                (near, k, piece_owner(me, other, 0, 1, k)),
                (far, k, piece_owner(me, other, 1, 0, k)),
                (far, 4 + k, piece_owner(me, other, 1, 1, k)),
            ):
                for i, start, rows, column in cuts:
                    pltpu.make_async_copy(
                        ref.at[at, pl.ds(start, rows)],
                        outs[i].at[owner, :, pl.ds(column, D)],
                        sems.at[i],
                    ).start()
    for i, out in enumerate(outs):
        pltpu.make_async_copy(out, out, sems.at[i]).wait()


def unpack(me, pieces, sizes, name):
    cuts = []
    start = 0
    for i, (rows, columns) in enumerate(sizes):
        for column in range(0, columns, D):
            cuts.append((i, start, rows, column))
            start += rows
    anywhere = pl.BlockSpec(memory_space=pl.ANY)
    return pl.pallas_call(
        functools.partial(unpack_kernel, tuple(cuts)),
        grid_spec=pltpu.PrefetchScalarGridSpec(
            num_scalar_prefetch=1,
            grid=(1,),
            in_specs=[anywhere] * 6,
            out_specs=[anywhere] * len(sizes),
            scratch_shapes=[pltpu.SemaphoreType.DMA((len(sizes),))],
        ),
        out_shape=[pltpu.VMEM((32, *size), BF) for size in sizes],
        compiler_params=pltpu.CompilerParams(vmem_limit_bytes=4 << 20),
        cost_estimate=pl.CostEstimate(
            flops=0, bytes_accessed=2 * 64 * D * start, transcendentals=0
        ),
        name=name,
    )(me, *pieces)


def place(me, total, keep, send, at):
    for other, target in ((0, keep), (1, send)):
        for far in (0, 1):
            for near in (0, 1):
                for k in range(4):
                    owner = piece_owner(me, other, far, near, k)
                    rows = total[pl.ds(pl.multiple_of(24 * owner, 8), 24), :]
                    at(target, 8 * far + 4 * near + k, rows.astype(BF))


def dw_expand_kernel(me_ref, fl_ref, ge_ref, c_ref, ga_ref, keep, send, total):
    j = pl.program_id(0)

    @pl.when(j < 4)
    def _():
        total[...] = tn(fl_ref[...], ge_ref[...])

    @pl.when(j == 4)
    def _():
        total[...] = tn(c_ref[...], ga_ref[...])

    def at(ref, piece, rows):
        ref[piece, 0] = rows

    place(me_ref[0], total, keep, send, at)


def dw_expand_packed(me, first_low, grad_expand, context, grad_attended):
    R = first_low.shape[0]
    fixed = pl.BlockSpec((R, D), lambda j, *_: (0, 0), pipeline_mode=pl.Buffered(1))
    out = pl.BlockSpec((16, 1, 24, D), lambda j, *_: (0, j, 0, 0))
    return pl.pallas_call(
        dw_expand_kernel,
        grid_spec=pltpu.PrefetchScalarGridSpec(
            num_scalar_prefetch=1,
            grid=(5,),
            in_specs=[
                fixed,
                pl.BlockSpec((R, D), lambda j, *_: (0, jnp.minimum(j, 3))),
                fixed,
                fixed,
            ],
            out_specs=[out, out],
            scratch_shapes=[pltpu.VMEM((D, D), F32)],
        ),
        out_shape=[jax.ShapeDtypeStruct((16, 5, 24, D), BF)] * 2,
        compiler_params=pltpu.CompilerParams(vmem_limit_bytes=40 << 20),
        cost_estimate=pl.CostEstimate(
            flops=10 * R * D * D, bytes_accessed=22_000_000, transcendentals=0
        ),
        name="dw_expand",
    )(me, *hbm(first_low, grad_expand, context, grad_attended))


def dw_shrink_kernel(me_ref, a_ref, gs_ref, keep, send, total):
    me = me_ref[0]
    core = me & 1
    i = pl.program_id(0)
    total[...] = tn(a_ref[...], gs_ref[...])
    for pair in range(4):
        for other, target in ((0, keep), (1, send)):
            local = 2 * pair + (core ^ other)
            away = (8 * i + local) ^ me ^ other
            side = core ^ other
            near = (away >> (1 + side)) & 1
            far = (away >> (2 - side)) & 1
            piece = 8 * far + 4 * near + (away >> 3)
            rows = total[pl.ds(pl.multiple_of(96 * local, 8), 96), :].astype(BF)
            target[piece] = rows


def dw_shrink_packed(me, active, grad_shrink):
    R = active.shape[0]
    out = pl.BlockSpec((16, 96, D), lambda i, *_: (0, 0, 0))
    return pl.pallas_call(
        dw_shrink_kernel,
        grid_spec=pltpu.PrefetchScalarGridSpec(
            num_scalar_prefetch=1,
            grid=(4,),
            in_specs=[
                pl.BlockSpec((R, D), lambda i, *_: (0, i)),
                pl.BlockSpec((R, D), lambda i, *_: (0, 0), pipeline_mode=pl.Buffered(1)),
            ],
            out_specs=[out, out],
            scratch_shapes=[pltpu.VMEM((D, D), F32)],
        ),
        out_shape=[jax.ShapeDtypeStruct((16, 96, D), BF)] * 2,
        compiler_params=pltpu.CompilerParams(vmem_limit_bytes=40 << 20),
        cost_estimate=pl.CostEstimate(
            flops=8 * R * D * D, bytes_accessed=17_000_000, transcendentals=0
        ),
        name="dw_shrink",
    )(me, *hbm(active, grad_shrink))


def dw_qkv_kernel(me_ref, x_ref, d_ref, rows_ref, keep, send, total):
    me = me_ref[0]
    i = pl.program_id(0)
    total[...] = tn(x_ref[...], d_ref[0])
    for unit in range(3):

        @pl.when(i == unit)
        def _():
            def at(ref, piece, rows):
                ref[piece, 24 * unit : 24 * unit + 24] = rows

            place(me, total, keep, send, at)

    @pl.when(i == 2)
    def _():
        for other, target in ((0, keep), (1, send)):
            for far in (0, 1):
                for near in (0, 1):
                    for k in range(4):
                        owner = piece_owner(me, other, far, near, k)
                        target[8 * far + 4 * near + k, 72:80] = rows_ref[owner]


def dw_qkv_packed(me, tokens, grads, rows):
    R = tokens.shape[0]
    out = pl.BlockSpec((16, 80, D), lambda i, *_: (0, 0, 0))
    return pl.pallas_call(
        dw_qkv_kernel,
        grid_spec=pltpu.PrefetchScalarGridSpec(
            num_scalar_prefetch=1,
            grid=(3,),
            in_specs=[
                pl.BlockSpec((R, D), lambda i, *_: (0, 0), pipeline_mode=pl.Buffered(1)),
                pl.BlockSpec((1, R, D), lambda i, *_: (i, 0, 0)),
                pl.BlockSpec((32, 8, D), lambda i, *_: (0, 0, 0)),
            ],
            out_specs=[out, out],
            scratch_shapes=[pltpu.VMEM((D, D), F32)],
        ),
        out_shape=[jax.ShapeDtypeStruct((16, 80, D), BF)] * 2,
        compiler_params=pltpu.CompilerParams(vmem_limit_bytes=30 << 20),
        cost_estimate=pl.CostEstimate(
            flops=6 * R * D * D, bytes_accessed=13_000_000, transcendentals=0
        ),
        name="dw_qkv",
    )(me, *hbm(tokens, grads), rows)


def first_kernel(*refs):
    query, key, value, *vectors, expand, out = refs
    out[0:24] = query[...]
    out[24:48] = key[...]
    out[48:72] = value[...]
    out[72:80] = jnp.zeros((8, D), BF)
    for i, vector in enumerate(vectors):
        out[72 + i : 73 + i, 0:24] = vector[...]
    out[72:73, 128:224] = expand[...]


def first_block(query, key, value, vectors, expand):
    return pl.pallas_call(
        first_kernel,
        out_shape=jax.ShapeDtypeStruct((80, D), BF),
        name="first_block",
    )(query, key, value, *[v[None] for v in vectors], expand[None])


def add_up(*parts):
    total = parts[0].astype(F32)
    for part in parts[1:]:
        total = total + part.astype(F32)
    return total


def halves(kept, came):
    n = kept.shape[0] // 2
    return (
        add_up(kept[:n], came[:n]).astype(BF),
        add_up(kept[n:], came[n:]).astype(BF),
    )


def quarters(kept, came):
    return [add_up(kept[k], came[k]).astype(BF) for k in range(4)]


def lines_of(parts):
    return [parts[0]] + [exchange(parts[k], flip(32, 8 * k)) for k in (1, 2, 3)]


def body(
    tokens,
    buckets,
    lengths,
    w_query,
    w_key,
    w_value,
    w_output,
    bias_query,
    bias_value,
    bias_output,
    gain_first,
    shift_first,
    w_expand,
    bias_expand,
    w_shrink,
    bias_shrink,
    gain_second,
    shift_second,
    grad_out,
    count,
):
    slots = buckets.shape[0]
    half = slots // 2
    whole = lambda v: lax.all_gather(v, "dp", axis=0, tiled=True)
    short = (
        bias_output,
        gain_first,
        shift_first,
        bias_shrink,
        gain_second,
        shift_second,
        bias_query,
        bias_value,
    )
    tree = count == 32
    if tree:
        me = lax.axis_index("dp").astype(jnp.int32).reshape(1)
        block_a = first_block(w_query, w_key, w_value, short, bias_expand)
        block_b = jnp.concatenate(
            [w_output] + [w_expand[:, D * i : D * i + D] for i in range(4)]
        )
        line_a = along_z(block_a)
        line_a, block_b = together(line_a, block_b)
        near_a = near(line_a)
        line_b = along_z(block_b)
        line_a, near_a, line_b, block_c = together(line_a, near_a, line_b, w_shrink)
        far_a = far(jnp.concatenate([line_a, near_a]))
        near_b = near(line_b)
        line_c = along_z(block_c)
        line_a, near_a, far_a, line_b, near_b, line_c = together(
            line_a, near_a, far_a, line_b, near_b, line_c
        )
        full_query, full_key, full_value, rows = unpack(
            me, both_cores(line_a, near_a, far_a), ((24, D),) * 3 + ((8, D),), "unpack_qkv"
        )
        full_query, full_key, full_value = [
            w.reshape(D, D) for w in (full_query, full_key, full_value)
        ]
        vectors = rows[:, :, :24].transpose(1, 0, 2).reshape(8, D)
        full_bias_expand = rows[:, 0, 128:224].reshape(1, 4 * D)
        far_b_in = jnp.concatenate([line_b, near_b])
        vectors, full_bias_expand, far_b_in, line_c = together(
            vectors, full_bias_expand, far_b_in, line_c
        )
        far_b = far(far_b_in)
        near_c = near(line_c)
        q, k, v, context, ends = attn_fwd(
            lengths, tokens, full_query, full_key, full_value, vectors, 0, slots
        )
        far_b, near_c, context = together(far_b, near_c, context)
        far_c_in = jnp.concatenate([line_c, near_c])
        full_output, full_expand = unpack(
            me, both_cores(line_b, near_b, far_b), ((24, D), (24, 4 * D)), "unpack_expand"
        )
        far_c = far(far_c_in)
        full_output = full_output.reshape(D, D)
        full_expand = full_expand.reshape(D, 4 * D)
    else:
        full_query, full_key, full_value, full_output, full_expand, full_shrink = [
            whole(w) for w in (w_query, w_key, w_value, w_output, w_expand, w_shrink)
        ]
        vectors = jnp.stack([whole(v) for v in short])
        full_bias_expand = whole(bias_expand)[None]
        q, k, v, context, ends = attn_fwd(
            lengths, tokens, full_query, full_key, full_value, vectors, 0, slots
        )

    normed, root, first_low, active, slope = ffn_in(
        tokens, context, full_output, full_expand, vectors, full_bias_expand, slots
    )
    if tree:
        far_c, normed = together(far_c, normed)
        (full_shrink,) = unpack(
            me, both_cores(line_c, near_c, far_c), ((96, D),), "unpack_shrink"
        )
        full_shrink = full_shrink.reshape(4 * D, D)
    (
        layer_out,
        grad_shrink,
        grad_expand,
        grad_h1,
        grad_attended,
        grad_context,
        sums_a,
        d_bias_expand,
    ) = ffn_out(
        buckets,
        normed,
        root,
        active,
        slope,
        grad_out,
        full_output,
        full_expand,
        full_shrink,
        vectors,
    )
    if tree:
        keep_b, send_b = dw_expand_packed(me, first_low, grad_expand, context, grad_attended)
        keep_b, send_b, active, grad_context = together(keep_b, send_b, active, grad_context)
        came_b = exchange(send_b, flip(32, 1))
        keep_c, send_c = dw_shrink_packed(me, active, grad_shrink)
        keep_c, send_c, came_b, grad_context = together(keep_c, send_c, came_b, grad_context)
        stay_b, go_b = halves(keep_b, came_b)
        stay_b, go_b, send_c, grad_context = together(stay_b, go_b, send_c, grad_context)
        came_b = far(go_b)
        came_c = exchange(send_c, flip(32, 1))
        begun, sums_b = attn_bwd(lengths, q, k, v, context, ends, grad_context, 0, half)
        sums_b, came_b, came_c = together(sums_b, came_b, came_c)
        stay_b, go_b = halves(stay_b, came_b)
        stay_c, go_c = halves(keep_c, came_c)
        grad_context, sums_b, stay_b, stay_c, go_b, go_c = together(
            grad_context, sums_b, stay_b, stay_c, go_b, go_c
        )
        came_b = near(go_b)
        came_c = far(go_c)
        grads, sums_c = attn_bwd(
            lengths, q, k, v, context, ends, grad_context, half, slots, (begun,)
        )
        sums_c, came_b, came_c = together(sums_c, came_b, came_c)
        sums_c = sums_c + sums_b
        parts_b = quarters(stay_b, came_b)
        stay_c, go_c = halves(stay_c, came_c)
        rows = jnp.concatenate([sums_a[:6], sums_c[:2]])
        rows = rows.reshape(8, 32, 24).transpose(1, 0, 2)
        long_rows = d_bias_expand.reshape(32, 1, 96)
        rows = jnp.pad(rows, ((0, 0), (0, 0), (0, D - 24))) + jnp.pad(
            long_rows, ((0, 0), (0, 7), (128, D - 224))
        )
        rows = rows.astype(BF)
        rows, stay_c, go_c, *parts_b = together(rows, stay_c, go_c, *parts_b)
        came_c = near(go_c)
        lines_b = lines_of(parts_b)
        keep_a, send_a = dw_qkv_packed(me, tokens, grads, rows)
        keep_a, send_a, came_c, *lines_b = together(keep_a, send_a, came_c, *lines_b)
        came_a = exchange(send_a, flip(32, 1))
        parts_c = quarters(stay_c, came_c)
        came_a, *parts_c = together(came_a, *parts_c)
        stay_a, go_a = halves(keep_a, came_a)
        stay_a, go_a, grad_h1, *parts_c = together(stay_a, go_a, grad_h1, *parts_c)
        came_a = far(go_a)
        lines_c = lines_of(parts_c)
    else:
        dw_expand = grad_w(first_low, grad_expand, 768, 768, "dw_expand")
        dw_output = grad_w(context, grad_attended, 768, 384, "dw_output")
        dw_shrink = grad_w(active, grad_shrink, 768, 768, "dw_shrink")
        grads, sums_c = attn_bwd(
            lengths, q, k, v, context, ends, grad_context, 0, slots
        )
        dw_query, dw_key, dw_value = [
            grad_w(tokens, grads[i], 768, 384, "dw_qkv") for i in range(3)
        ]
        sums = [sums_a[i] for i in range(6)] + [sums_c[0], sums_c[1]]
    grad_tokens = grad_in(
        grad_h1, grads, full_query, full_key, full_value, slots
    )
    if tree:
        grad_tokens, came_a, *lines_c = together(grad_tokens, came_a, *lines_c)
        stay_a, go_a = halves(stay_a, came_a)
        stay_a, go_a = together(stay_a, go_a)
        came_a = near(go_a)
        sum_b = add_up(*lines_b)
        sum_c = add_up(*lines_c)
        sum_a = add_up(*lines_of(quarters(stay_a, came_a)))
        own_query, own_key, own_value = [sum_a[24 * i : 24 * i + 24] for i in range(3)]
        own_output = sum_b[4]
        own_expand = jnp.concatenate([sum_b[i] for i in range(4)], 1)
        own_shrink = sum_c
        own_rows = sum_a[72:]
        own_short = [own_rows[i, :24] for i in range(8)]
        own_bias_expand = own_rows[0, 128:224]
    else:
        owned = lambda v: lax.psum_scatter(
            v.astype(F32), "dp", scatter_dimension=0, tiled=True
        )
        own_query, own_key, own_value, own_output, own_expand, own_shrink = [
            owned(w)
            for w in (dw_query, dw_key, dw_value, dw_output, dw_expand, dw_shrink)
        ]
        own_short = [owned(v) for v in sums]
        own_bias_expand = owned(d_bias_expand[0])
    (
        own_bias_output,
        own_gain_first,
        own_shift_first,
        own_bias_shrink,
        own_gain_second,
        own_shift_second,
        own_bias_query,
        own_bias_value,
    ) = own_short
    return (
        layer_out,
        grad_tokens,
        own_query,
        own_key,
        own_value,
        own_output,
        own_bias_query,
        own_bias_value,
        own_bias_output,
        own_gain_first,
        own_shift_first,
        own_expand,
        own_bias_expand,
        own_shrink,
        own_bias_shrink,
        own_gain_second,
        own_shift_second,
    )


def solution(mesh):
    split = P("dp")
    wide = P("dp", None)
    return jax.shard_map(
        functools.partial(body, count=mesh.shape["dp"]),
        mesh=mesh,
        in_specs=(wide, split, split)
        + (wide,) * 4
        + (split,) * 5
        + (wide, split, wide, split, split, split, wide),
        out_specs=(wide,) * 6 + (split,) * 5 + (wide, split, wide, split, split, split),
        check_vma=False,
    )
```
